32 devices in a mesh: wide: 16 (over z, y, core), narrow: 2 (over x).
Axes of the slice: x: 2, y: 2, z: 4, core: 2. Of those that a mesh axis runs over, the one named last changes fastest.
Arguments:
- pressure: float32 [64, 512, 1024], P(('narrow', 'wide')), may hold values from -6 to 6
- relax_freq: float32 [2], replicated, may hold values from 4 to 64
- relax_depth: float32 [2], replicated, may hold values from 0.1 to 0.6
Outputs:
- advanced: float32 [64, 512, 1024], P(('narrow', 'wide'))
The draws below stay inside these ranges and needn't reach their ends.
All inputs are finite; a program needn't handle non-finite values.
Results may differ from the reference program's by a relative error of at most 0.000084.
Values sent between devices are 32-bit elements; how exact they have to be, the bound alone decides.
No kernel may reach another device: no remote copies, remote signals or barrier semaphores. Data moves between devices by JAX's collectives and lax.ppermute only.
A program may use at most 128 MiB of HBM per device.

```python
import math
import jax
import jax.numpy as jnp
from jax import lax

NY = 512
NT = 1024
SUBSTEPS = 3
NX = 64


def shard_levels(rng, shape, shards, smallest, high):
    gain, own = 1.0, jax.random.fold_in(rng, 6)
    for dim, shards_of in shards:
        steps = jnp.exp(jax.random.uniform(jax.random.fold_in(own, dim), (shards_of,), jnp.float32, smallest / len(shards), high / len(shards)))
        gain = gain * jnp.repeat(steps, shape[dim] // shards_of).reshape([-1 if axis == dim else 1 for axis in range(len(shape))])
    return gain


def scatter_about(stream_key, extent, deviation, most, split=(), kind=jnp.bfloat16):
    factor_of = shard_levels(stream_key, extent, split, -0.22, 0.18) if split else 1.0
    entries = jax.random.normal(stream_key, extent, jnp.float32) * deviation * factor_of
    return jnp.minimum(jnp.maximum(entries, -most), most).astype(kind)


def setup_inputs(seed: int = 0) -> dict:
    splits = jax.random.split(jax.random.key(seed), 4)
    return {
        "pressure": scatter_about(splits[0], (NX, NY, NT), 1.0, 6.0, ((0, 32),), jnp.float32),
        "relax_freq": jnp.clip(jnp.exp(jax.random.uniform(splits[1], (2,), jnp.float32, math.log(4.0), math.log(64.0))), 4.0, 64.0),
        "relax_depth": jnp.clip(jnp.exp(jax.random.uniform(splits[2], (2,), jnp.float32, math.log(0.1), math.log(0.6))), 0.1, 0.6),
    }


WAVE_BREAKING = 0.1
RATE_TOP = 0.2


def burgers(acoustic_signal):
    squared = acoustic_signal * acoustic_signal
    bordered_signal = jnp.pad(squared, [(0, 0)] * (acoustic_signal.ndim - 1) + [(1, 1)])
    return acoustic_signal + WAVE_BREAKING * 0.25 * (bordered_signal[..., 2:] - bordered_signal[..., :-2])


def relax_factor(bin_index, relax_freq, relax_depth):
    total_re = jnp.zeros_like(bin_index)
    imaginary_total = jnp.zeros_like(bin_index)
    for process in range(2):
        ratio = bin_index / relax_freq[process]
        scaled = relax_depth[process] / (1.0 + ratio * ratio)
        total_re = total_re + scaled * ratio * ratio
        imaginary_total = imaginary_total + scaled * ratio
    amplitude = jnp.exp(-total_re)
    return amplitude * jnp.cos(imaginary_total), -amplitude * jnp.sin(imaginary_total)


def transverse_laplace(acoustic_signal):
    bordered_signal = jnp.pad(acoustic_signal, 1)
    return bordered_signal[2:, 1:-1] + bordered_signal[:-2, 1:-1] + bordered_signal[1:-1, 2:] + bordered_signal[1:-1, :-2] - 4.0 * acoustic_signal


def reference(pressure, relax_freq, relax_depth):
    n_freq = NT // 2
    bin_index = jnp.arange(n_freq, dtype=jnp.float32)
    factor_re, factor_im = relax_factor(bin_index, relax_freq, relax_depth)

    def forward(row):
        spectrum = jnp.fft.rfft(burgers(row), axis=-1)[:, :n_freq]
        real_part = jnp.real(spectrum)
        imag_part = jnp.imag(spectrum)
        return (real_part * factor_re - imag_part * factor_im, real_part * factor_im + imag_part * factor_re)

    real_part, imag_part = lax.map(forward, pressure)
    real_part = jnp.transpose(real_part, (2, 0, 1))
    imag_part = jnp.transpose(imag_part, (2, 0, 1))
    half_bins = jnp.float32(n_freq // 2)
    bin_rate = RATE_TOP * jnp.minimum(bin_index, 1.0) * jnp.minimum(1.0, half_bins / jnp.maximum(bin_index, 1.0))

    def diffract(item):
        real_bin, imag_bin, rate = item
        for partial_advance in range(SUBSTEPS):
            real_bin = real_bin - rate * transverse_laplace(imag_bin)
            imag_bin = imag_bin + rate * transverse_laplace(real_bin)
        return real_bin, imag_bin

    real_part, imag_part = lax.map(diffract, (real_part, imag_part, bin_rate))
    real_part = jnp.transpose(real_part, (1, 2, 0))
    imag_part = jnp.transpose(imag_part, (1, 2, 0))

    def inverse(item):
        real_row, imag_row = item
        full = lax.complex(real_row, imag_row)
        bordered_signal = jnp.pad(full, ((0, 0), (0, 1)))
        return jnp.fft.irfft(bordered_signal, n=NT, axis=-1)

    return lax.map(inverse, (real_part, imag_part))
```

```python
import functools

import jax
import jax.numpy as jnp
import ml_dtypes
import numpy as np
from jax import lax
from jax.experimental import pallas as pl
from jax.experimental.pallas import tpu as pltpu
from jax.sharding import PartitionSpec as P

SUBSTEPS = 3
WAVE_BREAKING = 0.1
RATE_TOP = 0.2

GANG = 4
SERIES = 2 * SUBSTEPS
LANES = 128
VMEM_LIMIT = 20 * 1024 * 1024
CHUNKS = (((0, 0, 6),), ((0, 6, 2), (1, 0, 4)), ((1, 4, 4),))
MEMBER, ABOVE, BELOW = range(3)
SCALARS = 3
ORDER = ("D0", "D2", "E0", "E1", "E2", "C0", "C1", "C2", "I1", "I2")


def pieces_of(chunk, per_parity):
    unit = per_parity // 8
    return tuple((parity, unit * first, unit * count) for parity, first, count in chunk)


def split_high_low(table):
    high = table.astype(np.float32).astype(ml_dtypes.bfloat16)
    low = (table - high.astype(np.float64)).astype(ml_dtypes.bfloat16)
    return jnp.asarray(high), jnp.asarray(low)


def transform_tables(piece, per_parity, n_time):
    parity, first, count = piece
    member = np.arange(GANG)[:, None]
    bins = 2 * (member * per_parity + first + np.arange(count)) + parity
    half = n_time // 2
    angles = ((bins[..., None] * np.arange(half)) % n_time) * (2.0 * np.pi / n_time)
    weights = np.where(bins == 0, 1.0, 2.0)[..., None] / n_time
    forward = np.stack([np.cos(angles), -np.sin(angles)], axis=1)
    inverse = np.stack([np.cos(angles) * weights, -np.sin(angles) * weights], axis=1)
    return split_high_low(forward.reshape(-1, half)), split_high_low(inverse.reshape(-1, half))


def halves(values):
    high = values.astype(jnp.bfloat16)
    return high, (values - high.astype(jnp.float32)).astype(jnp.bfloat16)


def product(left, right, dims):
    dot = functools.partial(
        lax.dot_general, dimension_numbers=(dims, ((), ())), preferred_element_type=jnp.float32
    )
    return dot(left[0], right[0]) + (dot(left[0], right[1]) + dot(left[1], right[0]))


def partner_rows(table, member, count):
    rows = [
        table[pl.ds(pl.multiple_of((member ^ d) * 2 * count, 2 * count), 2 * count)]
        for d in range(GANG)
    ]
    return jnp.concatenate(rows, axis=0)


def pass_on(info, token):
    for place in range(SCALARS):
        token[place] = info[place]


def forward_kernel(chunks, per_parity, info, freq, depth, pressure, *refs):
    n_tables = 2 * sum(len(pieces) for pieces in chunks)
    tables = iter(refs[:n_tables])
    n_outs = GANG * len(chunks)
    outs = refs[n_tables : n_tables + n_outs]
    token = refs[n_tables + n_outs]
    factors = refs[n_tables + n_outs + 1 :]
    rows, block, n_time = pressure.shape
    half = n_time // 2
    member = info[MEMBER]
    pass_on(info, token)

    @pl.when(pl.program_id(0) == 0)
    def relaxation():
        for chunk, pieces in enumerate(chunks):
            share = factors[2 * chunk].shape[1]
            place = lax.broadcasted_iota(jnp.int32, (8, LANES * pl.cdiv(share, LANES)), 1)
            for d in range(GANG):
                bins = jnp.zeros(place.shape, jnp.int32)
                offset = 0
                for parity, first, count in pieces:
                    here = 2 * ((member ^ d) * per_parity + first - offset + place) + parity
                    bins = jnp.where(place >= offset, here, bins)
                    offset += count
                bins = bins.astype(jnp.float32)
                total_re = jnp.zeros(bins.shape, jnp.float32)
                total_im = jnp.zeros(bins.shape, jnp.float32)
                for process in range(2):
                    ratio = bins / freq[process]
                    scaled = depth[process] / (1.0 + ratio * ratio)
                    total_re = total_re + scaled * ratio * ratio
                    total_im = total_im + scaled * ratio
                amplitude = jnp.exp(-total_re)
                for part, values in enumerate(
                    (amplitude * jnp.cos(total_im), -amplitude * jnp.sin(total_im))
                ):
                    column = values.T[:share, :1]
                    factors[2 * chunk + part][d] = jnp.broadcast_to(column, (share, block))

    wave = pressure[...].reshape(rows * block, n_time)
    lane = lax.broadcasted_iota(jnp.int32, wave.shape, 1)
    squared = wave * wave
    after = jnp.where(lane == n_time - 1, 0.0, pltpu.roll(squared, n_time - 1, 1))
    before = jnp.where(lane == 0, 0.0, pltpu.roll(squared, 1, 1))
    steep = wave + WAVE_BREAKING * 0.25 * (after - before)
    early, late = steep[:, :half], steep[:, half:]
    folded = {}
    for parity in sorted(set(piece[0] for pieces in chunks for piece in pieces)):
        folded[parity] = halves(early - late if parity else early + late)
    for chunk, pieces in enumerate(chunks):
        factor_re, factor_im = factors[2 * chunk : 2 * chunk + 2]
        offset = 0
        for parity, first, count in pieces:
            table = [partner_rows(next(tables), member, count) for _ in range(2)]
            spectrum = product(table, folded[parity], ((1,), (1,)))
            spectrum = spectrum.reshape(GANG, 2, count, rows * block)
            for d in range(GANG):
                here = slice(offset, offset + count)
                fr, fi = factor_re[d, here], factor_im[d, here]
                out = outs[GANG * chunk + d]
                for row in range(rows):
                    across = slice(row * block, (row + 1) * block)
                    real, imag = spectrum[d, 0, :, across], spectrum[d, 1, :, across]
                    out[row, here] = real * fr - imag * fi
                    out[rows + row, here] = real * fi + imag * fr
            offset += count


def cost(microseconds):
    return pl.CostEstimate(
        flops=int(microseconds * 1153000000),
        bytes_accessed=int(microseconds * 3690000),
        transcendentals=0,
    )


def scalars():
    return pl.BlockSpec(memory_space=pltpu.SMEM)


def token_shape():
    return jax.ShapeDtypeStruct((SCALARS,), jnp.int32)


def in_hbm(array):
    return pltpu.with_memory_space_constraint(array, pltpu.HBM)


def forward_chunks(info, pressure, relax_freq, relax_depth, tables, chunks, per_parity):
    rows, width, n_time = pressure.shape
    flat = [in_hbm(t) for chunk in tables for pair in chunk for t in pair]
    out_specs, out_shape, scratch = [], [], []
    for pieces in chunks:
        share = sum(piece[2] for piece in pieces)
        block = pl.BlockSpec((2 * rows, share, LANES), lambda i: (0, 0, i))
        out_specs += [block] * GANG
        out_shape += [jax.ShapeDtypeStruct((2 * rows, share, width), jnp.float32)] * GANG
        scratch += [pltpu.VMEM((GANG, share, LANES), jnp.float32)] * 2
    outs = pl.pallas_call(
        functools.partial(forward_kernel, chunks, per_parity),
        grid=(width // LANES,),
        in_specs=[scalars()] * 3
        + [pl.BlockSpec((rows, LANES, n_time), lambda i: (0, i, 0))]
        + [pl.BlockSpec(t.shape, lambda i: (0, 0)) for t in flat],
        out_specs=out_specs + [scalars()],
        out_shape=out_shape + [token_shape()],
        scratch_shapes=scratch,
        compiler_params=pltpu.CompilerParams(vmem_limit_bytes=VMEM_LIMIT),
        cost_estimate=cost(2 + 2 * len(chunks)),
    )(info, relax_freq, relax_depth, in_hbm(pressure), *flat)
    return outs[-1], [outs[GANG * c : GANG * c + GANG] for c in range(len(chunks))]


def bin_rates(pieces, per_parity, member, half_bins, tile, shape):
    start, offset = 0, 0
    for parity, first, count in pieces:
        here = 2 * (member * per_parity + first + 8 * tile - offset) + parity
        start = jnp.where(8 * tile >= offset, here, start)
        offset += count
    bins = (start + 2 * lax.broadcasted_iota(jnp.int32, shape, 0)).astype(jnp.float32)
    return RATE_TOP * jnp.minimum(bins, 1.0) * jnp.minimum(1.0, half_bins / jnp.maximum(bins, 1.0))


def lateral(width):
    lane = lax.broadcasted_iota(jnp.int32, (8, LANES), 1)
    first_lane, last_lane = lane == 0, lane == LANES - 1

    def apply(center):
        pieces = [center[:, at : at + LANES] for at in range(0, width, LANES)]
        left = [0.0] + [pltpu.roll(piece, 1, 1) for piece in pieces]
        right = [pltpu.roll(piece, LANES - 1, 1) for piece in pieces] + [0.0]
        sides = [
            jnp.where(first_lane, left[n], left[n + 1])
            + jnp.where(last_lane, right[n + 1], right[n])
            - 4.0 * piece
            for n, piece in enumerate(pieces)
        ]
        return jnp.concatenate(sides, axis=1)

    return apply


def evolve_kernel(pieces, per_parity, half_bins, info, *refs):
    parts = refs[:GANG]
    done, top, bottom, token, real, imag = refs[GANG:]
    member = info[MEMBER]
    pass_on(info, token)
    units, share, width = parts[0].shape
    rows = units // 2
    count = GANG * rows
    side = lateral(width)

    def advance(field, other, scale):
        before, center = None, other[0]
        for row in range(count):
            after = other[row + 1] if row < count - 1 else None
            laplace = side(center)
            if before is not None:
                laplace = laplace + before
            if after is not None:
                laplace = laplace + after
            field[row] = field[row] + scale * laplace
            before, center = center, after

    def keep(place, here, field):
        top[place, here], bottom[place, here] = field[0], field[count - 1]

    def tile(index, carry):
        here = pl.ds(pl.multiple_of(8 * index, 8), 8)
        rate = bin_rates(pieces, per_parity, member, half_bins, index, (8, width))
        for d in range(GANG):
            first = (member ^ d) * rows
            for row in range(rows):
                real[first + row] = parts[d][row, here]
                imag[first + row] = parts[d][rows + row, here]
        for step in range(SUBSTEPS):
            keep(2 * step, here, imag)
            advance(real, imag, -rate)
            keep(2 * step + 1, here, real)
            advance(imag, real, rate)
        for row in range(count):
            done[row, here] = real[row]
            done[count + row, here] = imag[row]
        return carry

    lax.fori_loop(0, share // 8, tile, 0)


def in_vmem(count):
    return [pl.BlockSpec(memory_space=pltpu.VMEM)] * count


def evolve_chunk(info, parts, pieces, per_parity, half_bins):
    units, share, width = parts[0].shape
    count = GANG * units // 2
    scratch = pltpu.VMEM((count, 8, width), jnp.float32)
    sizes = (2 * count, SERIES, SERIES)
    return pl.pallas_call(
        functools.partial(evolve_kernel, pieces, per_parity, half_bins),
        in_specs=[scalars()] + in_vmem(GANG),
        out_specs=in_vmem(3) + [scalars()],
        out_shape=[jax.ShapeDtypeStruct((n, share, width), jnp.float32) for n in sizes]
        + [token_shape()],
        scratch_shapes=[scratch, scratch],
        compiler_params=pltpu.CompilerParams(vmem_limit_bytes=VMEM_LIMIT),
        cost_estimate=cost(3.0),
    )(info, *parts)


def correct_kernel(pieces, per_parity, half_bins, info, done, top, bottom, above, below, *refs):
    outs = refs[:GANG]
    token, total, near_re, near_im, far_re, far_im = refs[GANG:]
    member = info[MEMBER]
    pass_on(info, token)
    units, share, width = done.shape
    count = units // 2
    rows = count // GANG
    side = lateral(width)

    def advance(field, source, edge, scale, half_step, deep):
        before, center = edge, source[0] if half_step > 0 else None
        for row in range(deep):
            after = source[row + 1] if row + 1 < half_step else None
            around = before
            if center is not None:
                around = around + side(center)
            if after is not None:
                around = around + after
            change = scale * around
            field[row] = field[row] + change if row < half_step - 1 else change
            before, center = center, after

    def tile(index, carry):
        here = pl.ds(pl.multiple_of(8 * index, 8), 8)
        rate = bin_rates(pieces, per_parity, member, half_bins, index, (8, width))
        for unit in range(units):
            total[unit] = done[unit, here]
        for own, other, flag, order in (
            (top, above, info[ABOVE], range(count)),
            (bottom, below, info[BELOW], range(count - 1, -1, -1)),
        ):
            rate_far = rate * flag.astype(jnp.float32)
            for half_step in range(SERIES):
                own_edge, far_edge = own[half_step, here], other[half_step, here]
                near, near_from = (near_re, near_im) if half_step % 2 == 0 else (near_im, near_re)
                back, back_from = (far_re, far_im) if half_step % 2 == 0 else (far_im, far_re)
                sign = 1.0 if half_step % 2 else -1.0
                if half_step > 0:
                    own_edge = own_edge + near_from[0]
                    far_edge = far_edge + back_from[0]
                reach = min(half_step + 1, SERIES - 1 - half_step)
                advance(near, near_from, far_edge, sign * rate, half_step, half_step + 1)
                advance(back, back_from, own_edge, sign * rate_far, half_step, reach)
            for row in range(SERIES - 1):
                total[order[row]] = total[order[row]] + near_re[row]
            for row in range(SERIES):
                total[count + order[row]] = total[count + order[row]] + near_im[row]
        for d in range(GANG):
            first = (member ^ d) * rows
            for row in range(rows):
                outs[d][row, here] = total[first + row]
                outs[d][rows + row, here] = total[count + first + row]
        return carry

    lax.fori_loop(0, share // 8, tile, 0)


def correct_chunk(info, state, pieces, per_parity, half_bins):
    units, share, width = state[0].shape
    shape = jax.ShapeDtypeStruct((units // GANG, share, width), jnp.float32)
    strip = pltpu.VMEM((SERIES, 8, width), jnp.float32)
    return pl.pallas_call(
        functools.partial(correct_kernel, pieces, per_parity, half_bins),
        in_specs=[scalars()] + in_vmem(5),
        out_specs=in_vmem(GANG) + [scalars()],
        out_shape=[shape] * GANG + [token_shape()],
        scratch_shapes=[pltpu.VMEM((units, 8, width), jnp.float32)] + [strip] * 4,
        compiler_params=pltpu.CompilerParams(vmem_limit_bytes=VMEM_LIMIT),
        cost_estimate=cost(3.5),
    )(info, *state)


def inverse_kernel(chunks, held, last, info, *refs):
    n_parts = GANG * len(chunks)
    n_tables = 2 * sum(len(pieces) for pieces in chunks)
    parts, tables = refs[:n_parts], iter(refs[n_parts : n_parts + n_tables])
    refs = refs[n_parts + n_tables :]
    prior, outs, token = dict(zip(held, refs)), refs[len(held) : -1], refs[-1]
    member = info[MEMBER]
    rows, block = parts[0].shape[0] // 2, parts[0].shape[2]
    half = outs[0].shape[2] // 2 if last else outs[0].shape[2]
    pass_on(info, token)
    sums = {parity: prior[parity][...].reshape(rows * block, half) for parity in held}
    for chunk, pieces in enumerate(chunks):
        offset = 0
        for parity, first, count in pieces:
            pair = [partner_rows(next(tables), member, count) for _ in range(2)]
            here = slice(offset, offset + count)
            packed = [
                jnp.concatenate([part[n * rows + row, here] for row in range(rows)], axis=1)
                for part in parts[GANG * chunk : GANG * chunk + GANG]
                for n in range(2)
            ]
            packed = jnp.concatenate(packed, axis=0).T
            term = product(halves(packed), pair, ((1,), (0,)))
            sums[parity] = sums[parity] + term if parity in sums else term
            offset += count
    if last:
        outs[0][:, :, :half] = (sums[0] + sums[1]).reshape(rows, block, half)
        outs[0][:, :, half:] = (sums[0] - sums[1]).reshape(rows, block, half)
    else:
        for out, parity in zip(outs, sorted(sums)):
            out[...] = sums[parity].reshape(rows, block, half)


def inverse_chunks(info, parts, tables, chunks, sums, last):
    rows, width = parts[0][0].shape[0] // 2, parts[0][0].shape[2]
    half = tables[0][0][0].shape[1]
    flat = [t for chunk in tables for pair in chunk for t in pair]
    held = sorted(sums)
    fresh = sorted(set(held) | set(piece[0] for pieces in chunks for piece in pieces))
    state = pl.BlockSpec((rows, LANES, half), lambda i: (0, i, 0))
    state_shape = jax.ShapeDtypeStruct((rows, width, half), jnp.float32)
    if last:
        out_specs = [pl.BlockSpec((rows, LANES, 2 * half), lambda i: (0, i, 0))]
        out_shape = [jax.ShapeDtypeStruct((rows, width, 2 * half), jnp.float32)]
    else:
        out_specs, out_shape = [state] * len(fresh), [state_shape] * len(fresh)
    in_specs = [scalars()]
    for chunk in parts:
        in_specs += [pl.BlockSpec(chunk[0].shape[:2] + (LANES,), lambda i: (0, 0, i))] * GANG
    outs = pl.pallas_call(
        functools.partial(inverse_kernel, chunks, held, last),
        grid=(width // LANES,),
        in_specs=in_specs
        + [pl.BlockSpec(t.shape, lambda i: (0, 0)) for t in flat]
        + [state] * len(held),
        out_specs=out_specs + [scalars()],
        out_shape=out_shape + [token_shape()],
        compiler_params=pltpu.CompilerParams(vmem_limit_bytes=VMEM_LIMIT),
        cost_estimate=cost(2 + 2 * len(chunks)),
    )(info, *[part for chunk in parts for part in chunk], *flat, *[sums[p] for p in held])
    return outs[-1], outs[0] if last else dict(zip(fresh, outs))


def shards(narrow, wide, axes, pressure, relax_freq, relax_depth):
    rows, width, n_time = pressure.shape
    n_freq = n_time // 2
    per_parity = n_freq // (2 * GANG)
    half_bins = float(n_freq // 2)
    blocks = narrow * wide // GANG

    def device(block, member):
        n, w = divmod(block * GANG + member, wide)
        return w * narrow + n if axes[0] == "wide" else n * wide + w

    swaps = [
        [(device(b, m), device(b, m ^ d)) for b in range(blocks) for m in range(GANG)]
        for d in range(GANG)
    ]
    down = [(device(b, m), device(b + 1, m)) for b in range(blocks - 1) for m in range(GANG)]
    up = [(target, source) for source, target in down]

    place = lax.axis_index("narrow") * wide + lax.axis_index("wide")
    block = place // GANG
    info = [place % GANG, block > 0, block < blocks - 1]
    info = jnp.stack([jnp.asarray(value, jnp.int32) for value in info])

    def swap(parts):
        return [parts[0]] + [lax.ppermute(parts[d], axes, swaps[d]) for d in range(1, GANG)]

    chunks = [pieces_of(chunk, per_parity) for chunk in CHUNKS]
    tables = [[transform_tables(piece, per_parity, n_time) for piece in c] for c in chunks]
    forward = [[pair[0] for pair in c] for c in tables]
    inverse = [[pair[1] for pair in c] for c in tables]
    held = [None] * len(chunks)
    inputs = (pressure, relax_freq, relax_depth)
    sums, begun, finished = {}, 0, 0
    for kernel, c in [(step[0], int(step[1:])) for step in ORDER]:
        shape = (chunks[c], per_parity, half_bins)
        if kernel == "D":
            some, begun = slice(begun, c + 1), c + 1
            info, parts = forward_chunks(info, *inputs, forward[some], chunks[some], per_parity)
            held[some] = [swap(part) for part in parts]
        elif kernel == "E":
            done, top, bottom, info = evolve_chunk(info, held[c], *shape)
            above = lax.ppermute(bottom, axes, down)
            below = lax.ppermute(top, axes, up)
            held[c] = (done, top, bottom, above, below)
        elif kernel == "C":
            *parts, info = correct_chunk(info, held[c], *shape)
            held[c] = swap(parts)
        else:
            some, finished, last = slice(finished, c + 1), c + 1, c + 1 == len(chunks)
            info, sums = inverse_chunks(info, held[some], inverse[some], chunks[some], sums, last)
    return sums


def solution(mesh):
    narrow, wide = mesh.shape["narrow"], mesh.shape["wide"]
    placed = (P(("narrow", "wide"), None, None), P(), P())
    return jax.shard_map(
        functools.partial(shards, narrow, wide, tuple(mesh.axis_names)),
        mesh=mesh,
        in_specs=placed,
        out_specs=P(("narrow", "wide"), None, None),
        check_vma=False,
    )
```

```python
import functools

import jax
import jax.numpy as jnp
import ml_dtypes
import numpy as np
from jax import lax
from jax.experimental import pallas as pl
from jax.experimental.pallas import tpu as pltpu
from jax.sharding import PartitionSpec as P

SUBSTEPS = 3
WAVE_BREAKING = 0.1
RATE_TOP = 0.2

GANG = 4
SERIES = 2 * SUBSTEPS
LANES = 128
VMEM_LIMIT = 20 * 1024 * 1024
CHUNKS = (((0, 0, 4),), ((0, 4, 4),), ((1, 0, 4),), ((1, 4, 4),))
MEMBER, ABOVE, BELOW = range(3)
SCALARS = 3
ORDER = ("D1", "D3", "E0", "E1", "C0", "E2", "C1", "E3", "I0", "C2", "I1", "C3", "I2", "I3")


def pieces_of(chunk, per_parity):
    unit = per_parity // 8
    return tuple((parity, unit * first, unit * count) for parity, first, count in chunk)


def split_high_low(table):
    high = table.astype(np.float32).astype(ml_dtypes.bfloat16)
    low = (table - high.astype(np.float64)).astype(ml_dtypes.bfloat16)
    return jnp.asarray(high), jnp.asarray(low)


def transform_tables(piece, per_parity, n_time):
    parity, first, count = piece
    member = np.arange(GANG)[:, None]
    bins = 2 * (member * per_parity + first + np.arange(count)) + parity
    half = n_time // 2
    angles = ((bins[..., None] * np.arange(half)) % n_time) * (2.0 * np.pi / n_time)
    weights = np.where(bins == 0, 1.0, 2.0)[..., None] / n_time
    forward = np.stack([np.cos(angles), -np.sin(angles)], axis=1)
    inverse = np.stack([np.cos(angles) * weights, -np.sin(angles) * weights], axis=1)
    return split_high_low(forward.reshape(-1, half)), split_high_low(inverse.reshape(-1, half))


def halves(values):
    high = values.astype(jnp.bfloat16)
    return high, (values - high.astype(jnp.float32)).astype(jnp.bfloat16)


def product(left, right, dims):
    dot = functools.partial(
        lax.dot_general, dimension_numbers=(dims, ((), ())), preferred_element_type=jnp.float32
    )
    return dot(left[0], right[0]) + (dot(left[0], right[1]) + dot(left[1], right[0]))


def partner_rows(table, member, count):
    rows = [
        table[pl.ds(pl.multiple_of((member ^ d) * 2 * count, 2 * count), 2 * count)]
        for d in range(GANG)
    ]
    return jnp.concatenate(rows, axis=0)


def pass_on(info, token):
    for place in range(SCALARS):
        token[place] = info[place]


def forward_kernel(chunks, per_parity, info, freq, depth, pressure, *refs):
    n_tables = 2 * sum(len(pieces) for pieces in chunks)
    tables = iter(refs[:n_tables])
    n_outs = GANG * len(chunks)
    outs = refs[n_tables : n_tables + n_outs]
    token = refs[n_tables + n_outs]
    factors = refs[n_tables + n_outs + 1 :]
    rows, block, n_time = pressure.shape
    half = n_time // 2
    member = info[MEMBER]
    pass_on(info, token)

    @pl.when(pl.program_id(0) == 0)
    def relaxation():
        for chunk, pieces in enumerate(chunks):
            share = factors[2 * chunk].shape[1]
            place = lax.broadcasted_iota(jnp.int32, (8, LANES * pl.cdiv(share, LANES)), 1)
            for d in range(GANG):
                bins = jnp.zeros(place.shape, jnp.int32)
                offset = 0
                for parity, first, count in pieces:
                    here = 2 * ((member ^ d) * per_parity + first - offset + place) + parity
                    bins = jnp.where(place >= offset, here, bins)
                    offset += count
                bins = bins.astype(jnp.float32)
                total_re = jnp.zeros(bins.shape, jnp.float32)
                total_im = jnp.zeros(bins.shape, jnp.float32)
                for process in range(2):
                    ratio = bins / freq[process]
                    scaled = depth[process] / (1.0 + ratio * ratio)
                    total_re = total_re + scaled * ratio * ratio
                    total_im = total_im + scaled * ratio
                amplitude = jnp.exp(-total_re)
                for part, values in enumerate(
                    (amplitude * jnp.cos(total_im), -amplitude * jnp.sin(total_im))
                ):
                    column = values.T[:share, :1]
                    factors[2 * chunk + part][d] = jnp.broadcast_to(column, (share, block))

    wave = pressure[...].reshape(rows * block, n_time)
    lane = lax.broadcasted_iota(jnp.int32, wave.shape, 1)
    squared = wave * wave
    after = jnp.where(lane == n_time - 1, 0.0, pltpu.roll(squared, n_time - 1, 1))
    before = jnp.where(lane == 0, 0.0, pltpu.roll(squared, 1, 1))
    steep = wave + WAVE_BREAKING * 0.25 * (after - before)
    early, late = steep[:, :half], steep[:, half:]
    folded = {}
    for parity in sorted(set(piece[0] for pieces in chunks for piece in pieces)):
        folded[parity] = halves(early - late if parity else early + late)
    for chunk, pieces in enumerate(chunks):
        factor_re, factor_im = factors[2 * chunk : 2 * chunk + 2]
        offset = 0
        for parity, first, count in pieces:
            table = [partner_rows(next(tables), member, count) for _ in range(2)]
            spectrum = product(table, folded[parity], ((1,), (1,)))
            spectrum = spectrum.reshape(GANG, 2, count, rows * block)
            for d in range(GANG):
                here = slice(offset, offset + count)
                fr, fi = factor_re[d, here], factor_im[d, here]
                out = outs[GANG * chunk + d]
                for row in range(rows):
                    across = slice(row * block, (row + 1) * block)
                    real, imag = spectrum[d, 0, :, across], spectrum[d, 1, :, across]
                    out[row, here] = real * fr - imag * fi
                    out[rows + row, here] = real * fi + imag * fr
            offset += count


def cost(microseconds):
    return pl.CostEstimate(
        flops=int(microseconds * 1153000),
        bytes_accessed=int(microseconds * 3690000),
        transcendentals=0,
    )


def scalars():
    return pl.BlockSpec(memory_space=pltpu.SMEM)


def token_shape():
    return jax.ShapeDtypeStruct((SCALARS,), jnp.int32)


def in_hbm(array):
    return pltpu.with_memory_space_constraint(array, pltpu.HBM)


def forward_chunks(info, pressure, relax_freq, relax_depth, tables, chunks, per_parity):
    rows, width, n_time = pressure.shape
    flat = [in_hbm(t) for chunk in tables for pair in chunk for t in pair]
    out_specs, out_shape, scratch = [], [], []
    for pieces in chunks:
        share = sum(piece[2] for piece in pieces)
        block = pl.BlockSpec((2 * rows, share, LANES), lambda i: (0, 0, i))
        out_specs += [block] * GANG
        out_shape += [jax.ShapeDtypeStruct((2 * rows, share, width), jnp.float32)] * GANG
        scratch += [pltpu.VMEM((GANG, share, LANES), jnp.float32)] * 2
    outs = pl.pallas_call(
        functools.partial(forward_kernel, chunks, per_parity),
        grid=(width // LANES,),
        in_specs=[scalars()] * 3
        + [pl.BlockSpec((rows, LANES, n_time), lambda i: (0, i, 0))]
        + [pl.BlockSpec(t.shape, lambda i: (0, 0)) for t in flat],
        out_specs=out_specs + [scalars()],
        out_shape=out_shape + [token_shape()],
        scratch_shapes=scratch,
        compiler_params=pltpu.CompilerParams(vmem_limit_bytes=VMEM_LIMIT),
        cost_estimate=cost(2 + 2 * len(chunks)),
    )(info, relax_freq, relax_depth, in_hbm(pressure), *flat)
    return outs[-1], [outs[GANG * c : GANG * c + GANG] for c in range(len(chunks))]


def bin_rates(pieces, per_parity, member, half_bins, tile, shape):
    start, offset = 0, 0
    for parity, first, count in pieces:
        here = 2 * (member * per_parity + first + 8 * tile - offset) + parity
        start = jnp.where(8 * tile >= offset, here, start)
        offset += count
    bins = (start + 2 * lax.broadcasted_iota(jnp.int32, shape, 0)).astype(jnp.float32)
    return RATE_TOP * jnp.minimum(bins, 1.0) * jnp.minimum(1.0, half_bins / jnp.maximum(bins, 1.0))


def lateral(width):
    lane = lax.broadcasted_iota(jnp.int32, (8, LANES), 1)
    first_lane, last_lane = lane == 0, lane == LANES - 1

    def apply(center):
        pieces = [center[:, at : at + LANES] for at in range(0, width, LANES)]
        left = [0.0] + [pltpu.roll(piece, 1, 1) for piece in pieces]
        right = [pltpu.roll(piece, LANES - 1, 1) for piece in pieces] + [0.0]
        sides = [
            jnp.where(first_lane, left[n], left[n + 1])
            + jnp.where(last_lane, right[n + 1], right[n])
            - 4.0 * piece
            for n, piece in enumerate(pieces)
        ]
        return jnp.concatenate(sides, axis=1)

    return apply


def evolve_kernel(pieces, per_parity, half_bins, info, *refs):
    parts = refs[:GANG]
    done, top, bottom, token, real, imag = refs[GANG:]
    member = info[MEMBER]
    pass_on(info, token)
    units, share, width = parts[0].shape
    rows = units // 2
    count = GANG * rows
    side = lateral(width)

    def advance(field, other, scale):
        before, center = None, other[0]
        for row in range(count):
            after = other[row + 1] if row < count - 1 else None
            laplace = side(center)
            if before is not None:
                laplace = laplace + before
            if after is not None:
                laplace = laplace + after
            field[row] = field[row] + scale * laplace
            before, center = center, after

    def keep(place, here, field):
        top[place, here], bottom[place, here] = field[0], field[count - 1]

    def tile(index, carry):
        here = pl.ds(pl.multiple_of(8 * index, 8), 8)
        rate = bin_rates(pieces, per_parity, member, half_bins, index, (8, width))
        for d in range(GANG):
            first = (member ^ d) * rows
            for row in range(rows):
                real[first + row] = parts[d][row, here]
                imag[first + row] = parts[d][rows + row, here]
        for step in range(SUBSTEPS):
            keep(2 * step, here, imag)
            advance(real, imag, -rate)
            keep(2 * step + 1, here, real)
            advance(imag, real, rate)
        for row in range(count):
            done[row, here] = real[row]
            done[count + row, here] = imag[row]
        return carry

    lax.fori_loop(0, share // 8, tile, 0)


def in_vmem(count):
    return [pl.BlockSpec(memory_space=pltpu.VMEM)] * count


def evolve_chunk(info, parts, pieces, per_parity, half_bins):
    units, share, width = parts[0].shape
    count = GANG * units // 2
    scratch = pltpu.VMEM((count, 8, width), jnp.float32)
    sizes = (2 * count, SERIES, SERIES)
    return pl.pallas_call(
        functools.partial(evolve_kernel, pieces, per_parity, half_bins),
        in_specs=[scalars()] + in_vmem(GANG),
        out_specs=in_vmem(3) + [scalars()],
        out_shape=[jax.ShapeDtypeStruct((n, share, width), jnp.float32) for n in sizes]
        + [token_shape()],
        scratch_shapes=[scratch, scratch],
        compiler_params=pltpu.CompilerParams(vmem_limit_bytes=VMEM_LIMIT),
        cost_estimate=cost(3.0),
    )(info, *parts)


def correct_kernel(pieces, per_parity, half_bins, info, done, top, bottom, above, below, *refs):
    outs = refs[:GANG]
    token, total, near_re, near_im, far_re, far_im = refs[GANG:]
    member = info[MEMBER]
    pass_on(info, token)
    units, share, width = done.shape
    count = units // 2
    rows = count // GANG
    side = lateral(width)

    def advance(field, source, edge, scale, half_step, deep):
        before, center = edge, source[0] if half_step > 0 else None
        for row in range(deep):
            after = source[row + 1] if row + 1 < half_step else None
            around = before
            if center is not None:
                around = around + side(center)
            if after is not None:
                around = around + after
            change = scale * around
            field[row] = field[row] + change if row < half_step - 1 else change
            before, center = center, after

    def tile(index, carry):
        here = pl.ds(pl.multiple_of(8 * index, 8), 8)
        rate = bin_rates(pieces, per_parity, member, half_bins, index, (8, width))
        for unit in range(units):
            total[unit] = done[unit, here]
        for own, other, flag, order in (
            (top, above, info[ABOVE], range(count)),
            (bottom, below, info[BELOW], range(count - 1, -1, -1)),
        ):
            rate_far = rate * flag.astype(jnp.float32)
            for half_step in range(SERIES):
                own_edge, far_edge = own[half_step, here], other[half_step, here]
                near, near_from = (near_re, near_im) if half_step % 2 == 0 else (near_im, near_re)
                back, back_from = (far_re, far_im) if half_step % 2 == 0 else (far_im, far_re)
                sign = 1.0 if half_step % 2 else -1.0
                if half_step > 0:
                    own_edge = own_edge + near_from[0]
                    far_edge = far_edge + back_from[0]
                reach = min(half_step + 1, SERIES - 1 - half_step)
                advance(near, near_from, far_edge, sign * rate, half_step, half_step + 1)
                advance(back, back_from, own_edge, sign * rate_far, half_step, reach)
            for row in range(SERIES - 1):
                total[order[row]] = total[order[row]] + near_re[row]
            for row in range(SERIES):
                total[count + order[row]] = total[count + order[row]] + near_im[row]
        for d in range(GANG):
            first = (member ^ d) * rows
            for row in range(rows):
                outs[d][row, here] = total[first + row]
                outs[d][rows + row, here] = total[count + first + row]
        return carry

    lax.fori_loop(0, share // 8, tile, 0)


def correct_chunk(info, state, pieces, per_parity, half_bins):
    units, share, width = state[0].shape
    shape = jax.ShapeDtypeStruct((units // GANG, share, width), jnp.float32)
    strip = pltpu.VMEM((SERIES, 8, width), jnp.float32)
    return pl.pallas_call(
        functools.partial(correct_kernel, pieces, per_parity, half_bins),
        in_specs=[scalars()] + in_vmem(5),
        out_specs=in_vmem(GANG) + [scalars()],
        out_shape=[shape] * GANG + [token_shape()],
        scratch_shapes=[pltpu.VMEM((units, 8, width), jnp.float32)] + [strip] * 4,
        compiler_params=pltpu.CompilerParams(vmem_limit_bytes=VMEM_LIMIT),
        cost_estimate=cost(3.5),
    )(info, *state)


def inverse_kernel(chunks, held, last, info, *refs):
    n_parts = GANG * len(chunks)
    n_tables = 2 * sum(len(pieces) for pieces in chunks)
    parts, tables = refs[:n_parts], iter(refs[n_parts : n_parts + n_tables])
    refs = refs[n_parts + n_tables :]
    prior, outs, token = dict(zip(held, refs)), refs[len(held) : -1], refs[-1]
    member = info[MEMBER]
    rows, block = parts[0].shape[0] // 2, parts[0].shape[2]
    half = outs[0].shape[2] // 2 if last else outs[0].shape[2]
    pass_on(info, token)
    sums = {parity: prior[parity][...].reshape(rows * block, half) for parity in held}
    for chunk, pieces in enumerate(chunks):
        offset = 0
        for parity, first, count in pieces:
            pair = [partner_rows(next(tables), member, count) for _ in range(2)]
            here = slice(offset, offset + count)
            packed = [
                jnp.concatenate([part[n * rows + row, here] for row in range(rows)], axis=1)
                for part in parts[GANG * chunk : GANG * chunk + GANG]
                for n in range(2)
            ]
            packed = jnp.concatenate(packed, axis=0).T
            term = product(halves(packed), pair, ((1,), (0,)))
            sums[parity] = sums[parity] + term if parity in sums else term
            offset += count
    if last:
        outs[0][:, :, :half] = (sums[0] + sums[1]).reshape(rows, block, half)
        outs[0][:, :, half:] = (sums[0] - sums[1]).reshape(rows, block, half)
    else:
        for out, parity in zip(outs, sorted(sums)):
            out[...] = sums[parity].reshape(rows, block, half)


def inverse_chunks(info, parts, tables, chunks, sums, last):
    rows, width = parts[0][0].shape[0] // 2, parts[0][0].shape[2]
    half = tables[0][0][0].shape[1]
    flat = [t for chunk in tables for pair in chunk for t in pair]
    held = sorted(sums)
    fresh = sorted(set(held) | set(piece[0] for pieces in chunks for piece in pieces))
    state = pl.BlockSpec((rows, LANES, half), lambda i: (0, i, 0))
    state_shape = jax.ShapeDtypeStruct((rows, width, half), jnp.float32)
    if last:
        out_specs = [pl.BlockSpec((rows, LANES, 2 * half), lambda i: (0, i, 0))]
        out_shape = [jax.ShapeDtypeStruct((rows, width, 2 * half), jnp.float32)]
    else:
        out_specs, out_shape = [state] * len(fresh), [state_shape] * len(fresh)
    in_specs = [scalars()]
    for chunk in parts:
        in_specs += [pl.BlockSpec(chunk[0].shape[:2] + (LANES,), lambda i: (0, 0, i))] * GANG
    outs = pl.pallas_call(
        functools.partial(inverse_kernel, chunks, held, last),
        grid=(width // LANES,),
        in_specs=in_specs
        + [pl.BlockSpec(t.shape, lambda i: (0, 0)) for t in flat]
        + [state] * len(held),
        out_specs=out_specs + [scalars()],
        out_shape=out_shape + [token_shape()],
        compiler_params=pltpu.CompilerParams(vmem_limit_bytes=VMEM_LIMIT),
        cost_estimate=cost(2 + 2 * len(chunks)),
    )(info, *[part for chunk in parts for part in chunk], *flat, *[sums[p] for p in held])
    return outs[-1], outs[0] if last else dict(zip(fresh, outs))


def shards(narrow, wide, axes, pressure, relax_freq, relax_depth):
    rows, width, n_time = pressure.shape
    n_freq = n_time // 2
    per_parity = n_freq // (2 * GANG)
    half_bins = float(n_freq // 2)
    blocks = narrow * wide // GANG

    def device(block, member):
        n, w = divmod(block * GANG + member, wide)
        return w * narrow + n if axes[0] == "wide" else n * wide + w

    swaps = [
        [(device(b, m), device(b, m ^ d)) for b in range(blocks) for m in range(GANG)]
        for d in range(GANG)
    ]
    down = [(device(b, m), device(b + 1, m)) for b in range(blocks - 1) for m in range(GANG)]
    up = [(target, source) for source, target in down]

    place = lax.axis_index("narrow") * wide + lax.axis_index("wide")
    block = place // GANG
    info = [place % GANG, block > 0, block < blocks - 1]
    info = jnp.stack([jnp.asarray(value, jnp.int32) for value in info])

    def swap(parts):
        return [parts[0]] + [lax.ppermute(parts[d], axes, swaps[d]) for d in range(1, GANG)]

    chunks = [pieces_of(chunk, per_parity) for chunk in CHUNKS]
    tables = [[transform_tables(piece, per_parity, n_time) for piece in c] for c in chunks]
    forward = [[pair[0] for pair in c] for c in tables]
    inverse = [[pair[1] for pair in c] for c in tables]
    held = [None] * len(chunks)
    inputs = (pressure, relax_freq, relax_depth)
    sums, begun, finished = {}, 0, 0
    for kernel, c in [(step[0], int(step[1:])) for step in ORDER]:
        shape = (chunks[c], per_parity, half_bins)
        if kernel == "D":
            some, begun = slice(begun, c + 1), c + 1
            info, parts = forward_chunks(info, *inputs, forward[some], chunks[some], per_parity)
            held[some] = [swap(part) for part in parts]
        elif kernel == "E":
            done, top, bottom, info = evolve_chunk(info, held[c], *shape)
            above = lax.ppermute(bottom, axes, down)
            below = lax.ppermute(top, axes, up)
            held[c] = (done, top, bottom, above, below)
        elif kernel == "C":
            *parts, info = correct_chunk(info, held[c], *shape)
            held[c] = swap(parts)
        else:
            some, finished, last = slice(finished, c + 1), c + 1, c + 1 == len(chunks)
            info, sums = inverse_chunks(info, held[some], inverse[some], chunks[some], sums, last)
    return sums


def solution(mesh):
    narrow, wide = mesh.shape["narrow"], mesh.shape["wide"]
    placed = (P(("narrow", "wide"), None, None), P(), P())
    return jax.shard_map(
        functools.partial(shards, narrow, wide, tuple(mesh.axis_names)),
        mesh=mesh,
        in_specs=placed,
        out_specs=P(("narrow", "wide"), None, None),
        check_vma=False,
    )
```

```python
import functools

import jax
import jax.numpy as jnp
import ml_dtypes
import numpy as np
from jax import lax
from jax.experimental import pallas as pl
from jax.experimental.pallas import tpu as pltpu
from jax.sharding import PartitionSpec as P

SUBSTEPS = 3
WAVE_BREAKING = 0.1
RATE_TOP = 0.2

GANG = 4
SERIES = 2 * SUBSTEPS
LANES = 128
WIDE = 256
VMEM_LIMIT = 20 * 1024 * 1024
CHUNKS = (((0, 0, 4),), ((0, 4, 4),), ((1, 0, 4),), ((1, 4, 4),))
MEMBER, ABOVE, BELOW, ODD = range(4)
SCALARS = 4
DIRECT_OUT, DIRECT_BACK = (0, 1, 2), (0, 1, 2, 3)
ORDER = ("D1", "D3", "E0", "E1", "R3", "C0", "E2", "C1", "E3", "I0", "C2", "I1", "C3", "I2", "I3")


def pieces_of(chunk, per_parity):
    unit = per_parity // 8
    return tuple((parity, unit * first, unit * count) for parity, first, count in chunk)


def split_high_low(table):
    high = table.astype(np.float32).astype(ml_dtypes.bfloat16)
    low = (table - high.astype(np.float64)).astype(ml_dtypes.bfloat16)
    return jnp.asarray(high), jnp.asarray(low)


def transform_tables(piece, per_parity, n_time):
    parity, first, count = piece
    member = np.arange(GANG)[:, None]
    bins = 2 * (member * per_parity + first + np.arange(count)) + parity
    half = n_time // 2
    angles = ((bins[..., None] * np.arange(half)) % n_time) * (2.0 * np.pi / n_time)
    weights = np.where(bins == 0, 1.0, 2.0)[..., None] / n_time
    forward = np.stack([np.cos(angles), -np.sin(angles)], axis=1)
    inverse = np.stack([np.cos(angles) * weights, -np.sin(angles) * weights], axis=1)
    return split_high_low(forward.reshape(-1, half)), split_high_low(inverse.reshape(-1, half))


def halves(values):
    high = values.astype(jnp.bfloat16)
    return high, (values - high.astype(jnp.float32)).astype(jnp.bfloat16)


def product(left, right, dims):
    dot = functools.partial(
        lax.dot_general, dimension_numbers=(dims, ((), ())), preferred_element_type=jnp.float32
    )
    return dot(left[0], right[0]) + (dot(left[0], right[1]) + dot(left[1], right[0]))


def sent_blocks(refs):
    if len(refs) == GANG:
        return list(refs)
    own, mates, pair = refs
    return [own, mates.at[0], pair.at[0], mates.at[1]]


def received_blocks(refs):
    if len(refs) == GANG:
        return list(refs)
    own, mates, pair = refs
    return [own, mates.at[0], pair.at[0], pair.at[1]]


def part_arrays(shape, block, over):
    doubled = (False, True, True) if over else (False,) * GANG
    shapes = [
        jax.ShapeDtypeStruct((2,) + shape if two else shape, jnp.float32) for two in doubled
    ]
    specs = [
        pl.BlockSpec(((2,) if two else ()) + block, lambda i, two=two: (0,) * (2 + two) + (i,))
        for two in doubled
    ]
    return shapes, specs


def split(refs, counts):
    places = [sum(counts[:n]) for n in range(len(counts) + 1)]
    return [list(refs[a:b]) for a, b in zip(places, places[1:])]


def partner_rows(table, member, count):
    rows = [
        table[pl.ds(pl.multiple_of((member ^ d) * 2 * count, 2 * count), 2 * count)]
        for d in range(GANG)
    ]
    return jnp.concatenate(rows, axis=0)


def pass_on(info, token):
    for place in range(SCALARS):
        token[place] = info[place]


def steepened_and_folded(wave, squared, parity):
    half = wave.shape[1] // 2
    sign = -1.0 if parity else 1.0

    def fold(values, at):
        return values[:, at : at + LANES] + sign * values[:, half + at : half + at + LANES]

    lane = lax.broadcasted_iota(jnp.int32, (wave.shape[0], LANES), 1)
    pieces = [fold(squared, at) for at in range(0, half, LANES)]
    last_early = sign * squared[:, half - LANES : half]
    first_late = squared[:, half : half + LANES]
    before = [pltpu.roll(piece, 1, 1) for piece in [last_early] + pieces]
    after = [pltpu.roll(piece, LANES - 1, 1) for piece in pieces + [first_late]]
    steep = [
        fold(wave, LANES * n)
        + WAVE_BREAKING
        * 0.25
        * (
            jnp.where(lane == LANES - 1, after[n + 1], after[n])
            - jnp.where(lane == 0, before[n], before[n + 1])
        )
        for n in range(half // LANES)
    ]
    return jnp.concatenate(steep, axis=1)


def forward_kernel(chunks, counts, per_parity, info, freq, depth, pressure, *refs):
    n_tables = 2 * sum(len(pieces) for pieces in chunks)
    tables = iter(refs[:n_tables])
    n_outs = sum(counts)
    outs = [sent_blocks(some) for some in split(refs[n_tables:], counts)]
    token = refs[n_tables + n_outs]
    factors = refs[n_tables + n_outs + 1 :]
    rows, block, n_time = pressure.shape
    half = n_time // 2
    member = info[MEMBER]
    pass_on(info, token)

    @pl.when(pl.program_id(0) == 0)
    def relaxation():
        for chunk, pieces in enumerate(chunks):
            share = factors[2 * chunk].shape[1]
            place = lax.broadcasted_iota(jnp.int32, (8, LANES * pl.cdiv(share, LANES)), 1)
            for d in range(GANG):
                bins = jnp.zeros(place.shape, jnp.int32)
                offset = 0
                for parity, first, count in pieces:
                    here = 2 * ((member ^ d) * per_parity + first - offset + place) + parity
                    bins = jnp.where(place >= offset, here, bins)
                    offset += count
                bins = bins.astype(jnp.float32)
                total_re = jnp.zeros(bins.shape, jnp.float32)
                total_im = jnp.zeros(bins.shape, jnp.float32)
                for process in range(2):
                    ratio = bins / freq[process]
                    scaled = depth[process] / (1.0 + ratio * ratio)
                    total_re = total_re + scaled * ratio * ratio
                    total_im = total_im + scaled * ratio
                amplitude = jnp.exp(-total_re)
                for part, values in enumerate(
                    (amplitude * jnp.cos(total_im), -amplitude * jnp.sin(total_im))
                ):
                    column = values.T[:share, :1]
                    factors[2 * chunk + part][d] = jnp.broadcast_to(column, (share, block))

    wave = pressure[...].reshape(rows * block, n_time)
    squared = wave * wave
    folded = {}
    for parity in sorted(set(piece[0] for pieces in chunks for piece in pieces)):
        folded[parity] = halves(steepened_and_folded(wave, squared, parity))
    for chunk, pieces in enumerate(chunks):
        factor_re, factor_im = factors[2 * chunk : 2 * chunk + 2]
        offset = 0
        for parity, first, count in pieces:
            table = [partner_rows(next(tables), member, count) for _ in range(2)]
            spectrum = product(table, folded[parity], ((1,), (1,)))
            spectrum = spectrum.reshape(GANG, 2, count, rows * block)
            for d in range(GANG):
                here = slice(offset, offset + count)
                fr, fi = factor_re[d, here], factor_im[d, here]
                out = outs[chunk][d]
                for row in range(rows):
                    across = slice(row * block, (row + 1) * block)
                    real, imag = spectrum[d, 0, :, across], spectrum[d, 1, :, across]
                    out[row, here] = real * fr - imag * fi
                    out[rows + row, here] = real * fi + imag * fr
            offset += count


def cost(microseconds):
    return pl.CostEstimate(
        flops=int(microseconds * 1153000),
        bytes_accessed=int(microseconds * 3690000),
        transcendentals=0,
    )


def scalars():
    return pl.BlockSpec(memory_space=pltpu.SMEM)


def token_shape():
    return jax.ShapeDtypeStruct((SCALARS,), jnp.int32)


def in_hbm(array):
    return pltpu.with_memory_space_constraint(array, pltpu.HBM)


def forward_chunks(info, pressure, relax_freq, relax_depth, tables, chunks, over, per_parity):
    rows, width, n_time = pressure.shape
    flat = [in_hbm(t) for chunk in tables for pair in chunk for t in pair]
    out_specs, out_shape, scratch = [], [], []
    counts = [3 if one else GANG for one in over]
    for pieces, one in zip(chunks, over):
        share = sum(piece[2] for piece in pieces)
        shape = (2 * rows, share)
        shapes, specs = part_arrays(shape + (width,), shape + (LANES,), one)
        out_specs += specs
        out_shape += shapes
        scratch += [pltpu.VMEM((GANG, share, LANES), jnp.float32)] * 2
    outs = pl.pallas_call(
        functools.partial(forward_kernel, chunks, counts, per_parity),
        grid=(width // LANES,),
        in_specs=[scalars()] * 3
        + [pl.BlockSpec((rows, LANES, n_time), lambda i: (0, i, 0))]
        + [pl.BlockSpec(t.shape, lambda i: (0, 0)) for t in flat],
        out_specs=out_specs + [scalars()],
        out_shape=out_shape + [token_shape()],
        scratch_shapes=scratch,
        compiler_params=pltpu.CompilerParams(vmem_limit_bytes=VMEM_LIMIT),
        cost_estimate=cost(2 + 2 * len(chunks)),
    )(info, in_hbm(relax_freq), in_hbm(relax_depth), in_hbm(pressure), *flat)
    return outs[-1], split(outs, counts)


def tile_of(share):
    return 16 if share % 16 == 0 else 8


def bin_rates(pieces, per_parity, member, half_bins, place, shape):
    start, offset = 0, 0
    for parity, first, count in pieces:
        here = 2 * (member * per_parity + first + place - offset) + parity
        start = jnp.where(place >= offset, here, start)
        offset += count
    bins = (start + 2 * lax.broadcasted_iota(jnp.int32, shape, 0)).astype(jnp.float32)
    return RATE_TOP * jnp.minimum(bins, 1.0) * jnp.minimum(1.0, half_bins / jnp.maximum(bins, 1.0))


def lateral(height, width):
    lane = lax.broadcasted_iota(jnp.int32, (height, LANES), 1)
    first_lane, last_lane = lane == 0, lane == LANES - 1

    def apply(center):
        pieces = [center[:, at : at + LANES] for at in range(0, width, LANES)]
        left = [0.0] + [pltpu.roll(piece, 1, 1) for piece in pieces]
        right = [pltpu.roll(piece, LANES - 1, 1) for piece in pieces] + [0.0]
        sides = [
            jnp.where(first_lane, left[n], left[n + 1])
            + jnp.where(last_lane, right[n + 1], right[n])
            - 4.0 * piece
            for n, piece in enumerate(pieces)
        ]
        return jnp.concatenate(sides, axis=1)

    return apply


def evolve_kernel(pieces, per_parity, half_bins, info, *refs):
    *parts, done, even_sent, odd_sent, token, real, imag = refs
    parts = received_blocks(parts)
    member, is_odd = info[MEMBER], info[ODD] != 0
    pass_on(info, token)
    units, share, width = parts[0].shape
    rows = units // 2
    count = GANG * rows
    height = tile_of(share)
    side = lateral(height, width)

    def advance(field, other, scale):
        before, center = None, other[0]
        for row in range(count):
            after = other[row + 1] if row < count - 1 else None
            laplace = side(center)
            if before is not None:
                laplace = laplace + before
            if after is not None:
                laplace = laplace + after
            field[row] = field[row] + scale * laplace
            before, center = center, after

    def keep(place, here, field):
        top, bottom = field[0], field[count - 1]
        even_sent[place, here] = jnp.where(is_odd, top, bottom)
        odd_sent[place, here] = jnp.where(is_odd, bottom, top)

    def tile(index, carry):
        place = pl.multiple_of(height * index, height)
        here = pl.ds(place, height)
        rate = bin_rates(pieces, per_parity, member, half_bins, place, (height, width))
        for d in range(GANG):
            first = (member ^ d) * rows
            for row in range(rows):
                real[first + row] = parts[d][row, here]
                imag[first + row] = parts[d][rows + row, here]
        for step in range(SUBSTEPS):
            keep(2 * step, here, imag)
            advance(real, imag, -rate)
            keep(2 * step + 1, here, real)
            advance(imag, real, rate)
        for row in range(count):
            done[row, here] = real[row]
            done[count + row, here] = imag[row]
        return carry

    lax.fori_loop(0, share // height, tile, 0)


def in_vmem(count):
    return [pl.BlockSpec(memory_space=pltpu.VMEM)] * count


def evolve_chunk(info, parts, pieces, per_parity, half_bins):
    units, share, width = parts[0].shape
    count = GANG * units // 2
    scratch = pltpu.VMEM((count, tile_of(share), width), jnp.float32)
    sizes = (2 * count, SERIES, SERIES)
    return pl.pallas_call(
        functools.partial(evolve_kernel, pieces, per_parity, half_bins),
        in_specs=[scalars()] + in_vmem(len(parts)),
        out_specs=in_vmem(3) + [scalars()],
        out_shape=[jax.ShapeDtypeStruct((n, share, width), jnp.float32) for n in sizes]
        + [token_shape()],
        scratch_shapes=[scratch, scratch],
        compiler_params=pltpu.CompilerParams(vmem_limit_bytes=VMEM_LIMIT),
        cost_estimate=cost(3.0),
    )(info, *parts)


def correct_kernel(
    pieces, per_parity, half_bins, info, done, even_sent, odd_sent, even_got, odd_got, *refs
):
    *outs, token, total = refs[:-8]
    outs, strips = sent_blocks(outs), refs[-8:]
    member, is_odd = info[MEMBER], info[ODD] != 0
    pass_on(info, token)
    units, share, width = done.shape
    count = units // 2
    rows = count // GANG
    height = tile_of(share)
    side = lateral(height, width)

    def advance(field, source, edge, scale, half_step, deep):
        before, center = edge, source[0] if half_step > 0 else None
        for row in range(deep):
            after = source[row + 1] if row + 1 < half_step else None
            around = before
            if center is not None:
                around = around + side(center)
            if after is not None:
                around = around + after
            change = scale * around
            field[row] = field[row] + change if row < half_step - 1 else change
            before, center = center, after

    def tile(index, carry):
        place = pl.multiple_of(height * index, height)
        here = pl.ds(place, height)
        rate = bin_rates(pieces, per_parity, member, half_bins, place, (height, width))
        for unit in range(units):
            total[unit] = done[unit, here]
        even, odd = (even_sent, even_got), (odd_sent, odd_got)
        edges = (
            (even, odd, info[ABOVE], strips[:4], range(count)),
            (odd, even, info[BELOW], strips[4:], range(count - 1, -1, -1)),
        )
        for half_step in range(SERIES):
            for if_odd, if_even, flag, (near_re, near_im, far_re, far_im), _ in edges:
                own_edge, far_edge = (
                    jnp.where(is_odd, one[half_step, here], two[half_step, here])
                    for one, two in zip(if_odd, if_even)
                )
                of_imag = half_step % 2
                near, near_from = (near_im, near_re) if of_imag else (near_re, near_im)
                far, far_from = (far_im, far_re) if of_imag else (far_re, far_im)
                scale = rate if of_imag else -rate
                if half_step > 0:
                    own_edge = own_edge + near_from[0]
                    far_edge = far_edge + far_from[0]
                back = min(half_step + 1, SERIES - 1 - half_step)
                advance(near, near_from, far_edge, scale, half_step, half_step + 1)
                scale = scale * flag.astype(jnp.float32)
                advance(far, far_from, own_edge, scale, half_step, back)
        for _, _, _, (near_re, near_im, _, _), order in edges:
            for row in range(SERIES - 1):
                total[order[row]] = total[order[row]] + near_re[row]
            for row in range(SERIES):
                total[count + order[row]] = total[count + order[row]] + near_im[row]
        for d in range(GANG):
            first = (member ^ d) * rows
            for row in range(rows):
                outs[d][row, here] = total[first + row]
                outs[d][rows + row, here] = total[count + first + row]
        return carry

    lax.fori_loop(0, share // height, tile, 0)


def correct_chunk(info, state, over, pieces, per_parity, half_bins):
    units, share, width = state[0].shape
    shape = (units // GANG, share, width)
    shapes = part_arrays(shape, shape, over)[0]
    strip = pltpu.VMEM((SERIES, tile_of(share), width), jnp.float32)
    return pl.pallas_call(
        functools.partial(correct_kernel, pieces, per_parity, half_bins),
        in_specs=[scalars()] + in_vmem(5),
        out_specs=in_vmem(len(shapes)) + [scalars()],
        out_shape=shapes + [token_shape()],
        scratch_shapes=[pltpu.VMEM((units, tile_of(share), width), jnp.float32)] + [strip] * 8,
        compiler_params=pltpu.CompilerParams(vmem_limit_bytes=VMEM_LIMIT),
        cost_estimate=cost(3.5),
    )(info, *state)


def relay_kernel(info, mates, held, pair, token):
    pair[1] = mates[1]
    pass_on(info, token)


def relay(info, mates, pair):
    return pl.pallas_call(
        relay_kernel,
        in_specs=[scalars()] + in_vmem(2),
        out_specs=in_vmem(1) + [scalars()],
        out_shape=[jax.ShapeDtypeStruct(pair.shape, pair.dtype), token_shape()],
        input_output_aliases={2: 0},
        compiler_params=pltpu.CompilerParams(vmem_limit_bytes=VMEM_LIMIT),
        cost_estimate=cost(0.5),
    )(info, mates, pair)


def inverse_kernel(chunks, counts, held, last, info, *refs):
    n_parts = sum(counts)
    n_tables = 2 * sum(len(pieces) for pieces in chunks)
    parts = [received_blocks(some) for some in split(refs, counts)]
    tables = iter(refs[n_parts : n_parts + n_tables])
    refs = refs[n_parts + n_tables :]
    prior, outs, token = dict(zip(held, refs)), refs[len(held) : -1], refs[-1]
    member = info[MEMBER]
    rows, block = parts[0][0].shape[0] // 2, parts[0][0].shape[2]
    half = outs[0].shape[2] // 2 if last else outs[0].shape[2]
    pass_on(info, token)
    sums = {parity: prior[parity][...].reshape(rows * block, half) for parity in held}
    for chunk, pieces in enumerate(chunks):
        offset = 0
        for parity, first, count in pieces:
            pair = [partner_rows(next(tables), member, count) for _ in range(2)]
            here = slice(offset, offset + count)
            packed = [
                jnp.concatenate([part[n * rows + row, here] for row in range(rows)], axis=1)
                for part in parts[chunk]
                for n in range(2)
            ]
            packed = jnp.concatenate(packed, axis=0).T
            term = product(halves(packed), pair, ((1,), (0,)))
            sums[parity] = sums[parity] + term if parity in sums else term
            offset += count
    if last:
        outs[0][:, :, :half] = (sums[0] + sums[1]).reshape(rows, block, half)
        outs[0][:, :, half:] = (sums[0] - sums[1]).reshape(rows, block, half)
    else:
        for out, parity in zip(outs, sorted(sums)):
            out[...] = sums[parity].reshape(rows, block, half)


def inverse_chunks(info, parts, tables, chunks, sums, last):
    rows, width = parts[0][0].shape[0] // 2, parts[0][0].shape[2]
    half = tables[0][0][0].shape[1]
    flat = [t for chunk in tables for pair in chunk for t in pair]
    held = sorted(sums)
    fresh = sorted(set(held) | set(piece[0] for pieces in chunks for piece in pieces))
    state = pl.BlockSpec((rows, WIDE, half), lambda i: (0, i, 0))
    state_shape = jax.ShapeDtypeStruct((rows, width, half), jnp.float32)
    if last:
        out_specs = [pl.BlockSpec((rows, WIDE, 2 * half), lambda i: (0, i, 0))]
        out_shape = [jax.ShapeDtypeStruct((rows, width, 2 * half), jnp.float32)]
    else:
        out_specs, out_shape = [state] * len(fresh), [state_shape] * len(fresh)
    in_specs = [scalars()]
    counts = [len(chunk) for chunk in parts]
    for chunk in parts:
        shape = chunk[0].shape
        in_specs += part_arrays(shape, shape[:2] + (WIDE,), len(chunk) == 3)[1]
    outs = pl.pallas_call(
        functools.partial(inverse_kernel, chunks, counts, held, last),
        grid=(width // WIDE,),
        in_specs=in_specs
        + [pl.BlockSpec(t.shape, lambda i: (0, 0)) for t in flat]
        + [state] * len(held),
        out_specs=out_specs + [scalars()],
        out_shape=out_shape + [token_shape()],
        compiler_params=pltpu.CompilerParams(vmem_limit_bytes=VMEM_LIMIT),
        cost_estimate=cost(2 + 2 * len(chunks)),
    )(info, *[part for chunk in parts for part in chunk], *flat, *[sums[p] for p in held])
    return outs[-1], outs[0] if last else dict(zip(fresh, outs))


def shards(narrow, wide, axes, pressure, relax_freq, relax_depth):
    rows, width, n_time = pressure.shape
    n_freq = n_time // 2
    per_parity = n_freq // (2 * GANG)
    half_bins = float(n_freq // 2)
    blocks = narrow * wide // GANG

    def device(block, member):
        n, w = divmod(block * GANG + member, wide)
        return w * narrow + n if axes[0] == "wide" else n * wide + w

    swaps = [
        [(device(b, m), device(b, m ^ d)) for b in range(blocks) for m in range(GANG)]
        for d in range(GANG)
    ]
    pairs = [
        [
            (device(b + side, m), device(b + 1 - side, m))
            for b in range(odd, blocks - 1, 2)
            for m in range(GANG)
            for side in range(2)
        ]
        for odd in range(2)
    ]

    place = lax.axis_index("narrow") * wide + lax.axis_index("wide")
    block = place // GANG
    info = [place % GANG, block > 0, block < blocks - 1, block % 2]
    info = jnp.stack([jnp.asarray(value, jnp.int32) for value in info])

    def swap(values, d):
        return lax.ppermute(values, axes, swaps[d])

    def send(parts):
        if len(parts) == GANG:
            return [parts[0]] + [swap(parts[d], d) for d in range(1, GANG)]
        own, mates, pair = parts
        return [own, swap(mates, 1), pair]

    chunks = [pieces_of(chunk, per_parity) for chunk in CHUNKS]
    tables = [[transform_tables(piece, per_parity, n_time) for piece in c] for c in chunks]
    forward = [[pair[0] for pair in c] for c in tables]
    inverse = [[pair[1] for pair in c] for c in tables]
    held = [None] * len(chunks)
    inputs = (pressure, relax_freq, relax_depth)
    sums, begun, finished = {}, 0, 0
    for kernel, c in [(step[0], int(step[1:])) for step in ORDER]:
        shape = (chunks[c], per_parity, half_bins)
        if kernel == "D":
            some, begun = slice(begun, c + 1), c + 1
            over = [n not in DIRECT_OUT for n in range(some.start, some.stop)]
            kind = (forward[some], chunks[some], over)
            info, parts = forward_chunks(info, *inputs, *kind, per_parity)
            held[some] = [send(part) for part in parts]
        elif kernel == "R":
            own, mates, pair = held[c]
            pair, info = relay(info, mates, pair)
            held[c] = [own, mates, swap(pair, 2)]
        elif kernel == "E":
            done, *sent, info = evolve_chunk(info, held[c], *shape)
            got = [lax.ppermute(values, axes, pairs[odd]) for odd, values in enumerate(sent)]
            held[c] = (done, *sent, *got)
        elif kernel == "C":
            *parts, info = correct_chunk(info, held[c], c not in DIRECT_BACK, *shape)
            held[c] = send(parts)
        else:
            some, finished, last = slice(finished, c + 1), c + 1, c + 1 == len(chunks)
            info, sums = inverse_chunks(info, held[some], inverse[some], chunks[some], sums, last)
    return sums


def solution(mesh):
    narrow, wide = mesh.shape["narrow"], mesh.shape["wide"]
    placed = (P(("narrow", "wide"), None, None), P(), P())
    return jax.shard_map(
        functools.partial(shards, narrow, wide, tuple(mesh.axis_names)),
        mesh=mesh,
        in_specs=placed,
        out_specs=P(("narrow", "wide"), None, None),
        check_vma=False,
    )
```

```python
import functools

import jax
import jax.numpy as jnp
import ml_dtypes
import numpy as np
from jax import lax
from jax.experimental import pallas as pl
from jax.experimental.pallas import tpu as pltpu
from jax.sharding import PartitionSpec as P

SUBSTEPS = 3
WAVE_BREAKING = 0.1
RATE_TOP = 0.2

GANG = 4
SERIES = 2 * SUBSTEPS
LANES = 128
WIDE = 256
VMEM_LIMIT = 20 * 1024 * 1024
CHUNKS = (((0, 0, 4),), ((0, 4, 4),), ((1, 0, 4),), ((1, 4, 4),))
MEMBER, ABOVE, BELOW, SECOND = range(4)
SCALARS = 4
ORDER = ("D1", "D3", "E0", "E1", "C0", "E2", "C1", "E3", "I0", "C2", "I1", "C3", "I2", "I3")


def pieces_of(chunk, per_parity):
    unit = per_parity // 8
    return tuple((parity, unit * first, unit * count) for parity, first, count in chunk)


def split_high_low(table):
    high = table.astype(np.float32).astype(ml_dtypes.bfloat16)
    low = (table - high.astype(np.float64)).astype(ml_dtypes.bfloat16)
    return jnp.asarray(high), jnp.asarray(low)


def transform_tables(piece, per_parity, n_time):
    parity, first, count = piece
    member = np.arange(GANG)[:, None]
    bins = 2 * (member * per_parity + first + np.arange(count)) + parity
    half = n_time // 2
    angles = ((bins[..., None] * np.arange(half)) % n_time) * (2.0 * np.pi / n_time)
    weights = np.where(bins == 0, 1.0, 2.0)[..., None] / n_time
    forward = np.stack([np.cos(angles), -np.sin(angles)], axis=1)
    inverse = np.stack([np.cos(angles) * weights, -np.sin(angles) * weights], axis=1)
    return split_high_low(forward.reshape(-1, half)), split_high_low(inverse.reshape(-1, half))


def halves(values):
    high = values.astype(jnp.bfloat16)
    return high, (values - high.astype(jnp.float32)).astype(jnp.bfloat16)


def product(left, right, dims):
    dot = functools.partial(
        lax.dot_general, dimension_numbers=(dims, ((), ())), preferred_element_type=jnp.float32
    )
    return dot(left[0], right[0]) + (dot(left[0], right[1]) + dot(left[1], right[0]))


def partner_rows(table, member, count):
    rows = [
        table[pl.ds(pl.multiple_of((member ^ d) * 2 * count, 2 * count), 2 * count)]
        for d in range(GANG)
    ]
    return jnp.concatenate(rows, axis=0)


def pass_on(info, token):
    for place in range(SCALARS):
        token[place] = info[place]


def steepened_and_folded(wave, squared, parity):
    half = wave.shape[1] // 2
    sign = -1.0 if parity else 1.0

    def fold(values, at):
        return values[:, at : at + LANES] + sign * values[:, half + at : half + at + LANES]

    lane = lax.broadcasted_iota(jnp.int32, (wave.shape[0], LANES), 1)
    pieces = [fold(squared, at) for at in range(0, half, LANES)]
    last_early = sign * squared[:, half - LANES : half]
    first_late = squared[:, half : half + LANES]
    before = [pltpu.roll(piece, 1, 1) for piece in [last_early] + pieces]
    after = [pltpu.roll(piece, LANES - 1, 1) for piece in pieces + [first_late]]
    steep = [
        fold(wave, LANES * n)
        + WAVE_BREAKING
        * 0.25
        * (
            jnp.where(lane == LANES - 1, after[n + 1], after[n])
            - jnp.where(lane == 0, before[n], before[n + 1])
        )
        for n in range(half // LANES)
    ]
    return jnp.concatenate(steep, axis=1)


def forward_kernel(chunks, per_parity, info, freq, depth, pressure, *refs):
    n_tables = 2 * sum(len(pieces) for pieces in chunks)
    tables = iter(refs[:n_tables])
    n_outs = GANG * len(chunks)
    outs = refs[n_tables : n_tables + n_outs]
    token = refs[n_tables + n_outs]
    factors = refs[n_tables + n_outs + 1 :]
    rows, block, n_time = pressure.shape
    half = n_time // 2
    member = info[MEMBER]
    pass_on(info, token)

    @pl.when(pl.program_id(0) == 0)
    def relaxation():
        for chunk, pieces in enumerate(chunks):
            share = factors[2 * chunk].shape[1]
            place = lax.broadcasted_iota(jnp.int32, (8, LANES * pl.cdiv(share, LANES)), 1)
            for d in range(GANG):
                bins = jnp.zeros(place.shape, jnp.int32)
                offset = 0
                for parity, first, count in pieces:
                    here = 2 * ((member ^ d) * per_parity + first - offset + place) + parity
                    bins = jnp.where(place >= offset, here, bins)
                    offset += count
                bins = bins.astype(jnp.float32)
                total_re = jnp.zeros(bins.shape, jnp.float32)
                total_im = jnp.zeros(bins.shape, jnp.float32)
                for process in range(2):
                    ratio = bins / freq[process]
                    scaled = depth[process] / (1.0 + ratio * ratio)
                    total_re = total_re + scaled * ratio * ratio
                    total_im = total_im + scaled * ratio
                amplitude = jnp.exp(-total_re)
                for part, values in enumerate(
                    (amplitude * jnp.cos(total_im), -amplitude * jnp.sin(total_im))
                ):
                    column = values.T[:share, :1]
                    factors[2 * chunk + part][d] = jnp.broadcast_to(column, (share, block))

    wave = pressure[...].reshape(rows * block, n_time)
    squared = wave * wave
    folded = {}
    for parity in sorted(set(piece[0] for pieces in chunks for piece in pieces)):
        folded[parity] = halves(steepened_and_folded(wave, squared, parity))
    for chunk, pieces in enumerate(chunks):
        factor_re, factor_im = factors[2 * chunk : 2 * chunk + 2]
        offset = 0
        for parity, first, count in pieces:
            table = [partner_rows(next(tables), member, count) for _ in range(2)]
            spectrum = product(table, folded[parity], ((1,), (1,)))
            spectrum = spectrum.reshape(GANG, 2, count, rows * block)
            for d in range(GANG):
                here = slice(offset, offset + count)
                fr, fi = factor_re[d, here], factor_im[d, here]
                out = outs[GANG * chunk + d]
                for row in range(rows):
                    across = slice(row * block, (row + 1) * block)
                    real, imag = spectrum[d, 0, :, across], spectrum[d, 1, :, across]
                    out[row, here] = real * fr - imag * fi
                    out[rows + row, here] = real * fi + imag * fr
            offset += count


def cost(microseconds):
    return pl.CostEstimate(
        flops=int(microseconds * 1153000),
        bytes_accessed=int(microseconds * 3690000),
        transcendentals=0,
    )


def scalars():
    return pl.BlockSpec(memory_space=pltpu.SMEM)


def token_shape():
    return jax.ShapeDtypeStruct((SCALARS,), jnp.int32)


def in_hbm(array):
    return pltpu.with_memory_space_constraint(array, pltpu.HBM)


def forward_chunks(info, pressure, relax_freq, relax_depth, tables, chunks, per_parity):
    rows, width, n_time = pressure.shape
    flat = [in_hbm(t) for chunk in tables for pair in chunk for t in pair]
    out_specs, out_shape, scratch = [], [], []
    for pieces in chunks:
        share = sum(piece[2] for piece in pieces)
        block = pl.BlockSpec((2 * rows, share, LANES), lambda i: (0, 0, i))
        out_specs += [block] * GANG
        out_shape += [jax.ShapeDtypeStruct((2 * rows, share, width), jnp.float32)] * GANG
        scratch += [pltpu.VMEM((GANG, share, LANES), jnp.float32)] * 2
    outs = pl.pallas_call(
        functools.partial(forward_kernel, chunks, per_parity),
        grid=(width // LANES,),
        in_specs=[scalars()] * 3
        + [pl.BlockSpec((rows, LANES, n_time), lambda i: (0, i, 0))]
        + [pl.BlockSpec(t.shape, lambda i: (0, 0)) for t in flat],
        out_specs=out_specs + [scalars()],
        out_shape=out_shape + [token_shape()],
        scratch_shapes=scratch,
        compiler_params=pltpu.CompilerParams(vmem_limit_bytes=VMEM_LIMIT),
        cost_estimate=cost(2 + 2 * len(chunks)),
    )(info, in_hbm(relax_freq), in_hbm(relax_depth), in_hbm(pressure), *flat)
    return outs[-1], [outs[GANG * c : GANG * c + GANG] for c in range(len(chunks))]


def tile_of(share):
    return 16 if share % 16 == 0 else 8


def bin_rates(pieces, per_parity, member, half_bins, place, shape):
    start, offset = 0, 0
    for parity, first, count in pieces:
        here = 2 * (member * per_parity + first + place - offset) + parity
        start = jnp.where(place >= offset, here, start)
        offset += count
    bins = (start + 2 * lax.broadcasted_iota(jnp.int32, shape, 0)).astype(jnp.float32)
    return RATE_TOP * jnp.minimum(bins, 1.0) * jnp.minimum(1.0, half_bins / jnp.maximum(bins, 1.0))


def lateral(height, width):
    lane = lax.broadcasted_iota(jnp.int32, (height, LANES), 1)
    first_lane, last_lane = lane == 0, lane == LANES - 1

    def apply(center):
        pieces = [center[:, at : at + LANES] for at in range(0, width, LANES)]
        left = [0.0] + [pltpu.roll(piece, 1, 1) for piece in pieces]
        right = [pltpu.roll(piece, LANES - 1, 1) for piece in pieces] + [0.0]
        sides = [
            jnp.where(first_lane, left[n], left[n + 1])
            + jnp.where(last_lane, right[n + 1], right[n])
            - 4.0 * piece
            for n, piece in enumerate(pieces)
        ]
        return jnp.concatenate(sides, axis=1)

    return apply


def evolve_kernel(pieces, per_parity, half_bins, info, *refs):
    parts = refs[:GANG]
    done, early_sent, late_sent, token, real, imag = refs[GANG:]
    member, is_second = info[MEMBER], info[SECOND] != 0
    pass_on(info, token)
    units, share, width = parts[0].shape
    rows = units // 2
    count = GANG * rows
    height = tile_of(share)
    side = lateral(height, width)

    def advance(field, other, scale):
        before, center = None, other[0]
        for row in range(count):
            after = other[row + 1] if row < count - 1 else None
            laplace = side(center)
            if before is not None:
                laplace = laplace + before
            if after is not None:
                laplace = laplace + after
            field[row] = field[row] + scale * laplace
            before, center = center, after

    def keep(place, here, field):
        top, bottom = field[0], field[count - 1]
        early_sent[place, here] = jnp.where(is_second, top, bottom)
        late_sent[place, here] = jnp.where(is_second, bottom, top)

    def tile(index, carry):
        place = pl.multiple_of(height * index, height)
        here = pl.ds(place, height)
        rate = bin_rates(pieces, per_parity, member, half_bins, place, (height, width))
        for d in range(GANG):
            first = (member ^ d) * rows
            for row in range(rows):
                real[first + row] = parts[d][row, here]
                imag[first + row] = parts[d][rows + row, here]
        for step in range(SUBSTEPS):
            keep(2 * step, here, imag)
            advance(real, imag, -rate)
            keep(2 * step + 1, here, real)
            advance(imag, real, rate)
        for row in range(count):
            done[row, here] = real[row]
            done[count + row, here] = imag[row]
        return carry

    lax.fori_loop(0, share // height, tile, 0)


def in_vmem(count):
    return [pl.BlockSpec(memory_space=pltpu.VMEM)] * count


def evolve_chunk(info, parts, pieces, per_parity, half_bins):
    units, share, width = parts[0].shape
    count = GANG * units // 2
    scratch = pltpu.VMEM((count, tile_of(share), width), jnp.float32)
    sizes = (2 * count, SERIES, SERIES)
    return pl.pallas_call(
        functools.partial(evolve_kernel, pieces, per_parity, half_bins),
        in_specs=[scalars()] + in_vmem(GANG),
        out_specs=in_vmem(3) + [scalars()],
        out_shape=[jax.ShapeDtypeStruct((n, share, width), jnp.float32) for n in sizes]
        + [token_shape()],
        scratch_shapes=[scratch, scratch],
        compiler_params=pltpu.CompilerParams(vmem_limit_bytes=VMEM_LIMIT),
        cost_estimate=cost(3.0),
    )(info, *parts)


def correct_kernel(
    pieces, per_parity, half_bins, info, done, early_sent, late_sent, early_got, late_got, *refs
):
    outs = refs[:GANG]
    token, total, *strips = refs[GANG:]
    member, is_second = info[MEMBER], info[SECOND] != 0
    pass_on(info, token)
    units, share, width = done.shape
    count = units // 2
    rows = count // GANG
    height = tile_of(share)
    side = lateral(height, width)

    def advance(field, source, edge, scale, half_step, deep):
        before, center = edge, source[0] if half_step > 0 else None
        for row in range(deep):
            after = source[row + 1] if row + 1 < half_step else None
            around = before
            if center is not None:
                around = around + side(center)
            if after is not None:
                around = around + after
            change = scale * around
            field[row] = field[row] + change if row < half_step - 1 else change
            before, center = center, after

    def tile(index, carry):
        place = pl.multiple_of(height * index, height)
        here = pl.ds(place, height)
        rate = bin_rates(pieces, per_parity, member, half_bins, place, (height, width))
        for unit in range(units):
            total[unit] = done[unit, here]
        early, late = (early_sent, early_got), (late_sent, late_got)
        edges = (
            (early, late, info[ABOVE], strips[:4], range(count)),
            (late, early, info[BELOW], strips[4:], range(count - 1, -1, -1)),
        )
        for half_step in range(SERIES):
            for if_second, if_first, flag, (near_re, near_im, far_re, far_im), _ in edges:
                own_edge, far_edge = (
                    jnp.where(is_second, one[half_step, here], two[half_step, here])
                    for one, two in zip(if_second, if_first)
                )
                of_imag = half_step % 2
                near, near_from = (near_im, near_re) if of_imag else (near_re, near_im)
                far, far_from = (far_im, far_re) if of_imag else (far_re, far_im)
                scale = rate if of_imag else -rate
                if half_step > 0:
                    own_edge = own_edge + near_from[0]
                    far_edge = far_edge + far_from[0]
                back = min(half_step + 1, SERIES - 1 - half_step)
                advance(near, near_from, far_edge, scale, half_step, half_step + 1)
                scale = scale * flag.astype(jnp.float32)
                advance(far, far_from, own_edge, scale, half_step, back)
        for _, _, _, (near_re, near_im, _, _), order in edges:
            for row in range(SERIES - 1):
                total[order[row]] = total[order[row]] + near_re[row]
            for row in range(SERIES):
                total[count + order[row]] = total[count + order[row]] + near_im[row]
        for d in range(GANG):
            first = (member ^ d) * rows
            for row in range(rows):
                outs[d][row, here] = total[first + row]
                outs[d][rows + row, here] = total[count + first + row]
        return carry

    lax.fori_loop(0, share // height, tile, 0)


def correct_chunk(info, state, pieces, per_parity, half_bins):
    units, share, width = state[0].shape
    shape = jax.ShapeDtypeStruct((units // GANG, share, width), jnp.float32)
    strip = pltpu.VMEM((SERIES, tile_of(share), width), jnp.float32)
    return pl.pallas_call(
        functools.partial(correct_kernel, pieces, per_parity, half_bins),
        in_specs=[scalars()] + in_vmem(5),
        out_specs=in_vmem(GANG) + [scalars()],
        out_shape=[shape] * GANG + [token_shape()],
        scratch_shapes=[pltpu.VMEM((units, tile_of(share), width), jnp.float32)] + [strip] * 8,
        compiler_params=pltpu.CompilerParams(vmem_limit_bytes=VMEM_LIMIT),
        cost_estimate=cost(3.5),
    )(info, *state)


def inverse_kernel(chunks, held, last, info, *refs):
    n_parts = GANG * len(chunks)
    n_tables = 2 * sum(len(pieces) for pieces in chunks)
    parts, tables = refs[:n_parts], iter(refs[n_parts : n_parts + n_tables])
    refs = refs[n_parts + n_tables :]
    prior, outs, token = dict(zip(held, refs)), refs[len(held) : -1], refs[-1]
    member = info[MEMBER]
    rows, block = parts[0].shape[0] // 2, parts[0].shape[2]
    half = outs[0].shape[2] // 2 if last else outs[0].shape[2]
    pass_on(info, token)
    sums = {parity: prior[parity][...].reshape(rows * block, half) for parity in held}
    for chunk, pieces in enumerate(chunks):
        offset = 0
        for parity, first, count in pieces:
            pair = [partner_rows(next(tables), member, count) for _ in range(2)]
            here = slice(offset, offset + count)
            packed = [
                jnp.concatenate([part[n * rows + row, here] for row in range(rows)], axis=1)
                for part in parts[GANG * chunk : GANG * chunk + GANG]
                for n in range(2)
            ]
            packed = jnp.concatenate(packed, axis=0).T
            term = product(halves(packed), pair, ((1,), (0,)))
            sums[parity] = sums[parity] + term if parity in sums else term
            offset += count
    if last:
        outs[0][:, :, :half] = (sums[0] + sums[1]).reshape(rows, block, half)
        outs[0][:, :, half:] = (sums[0] - sums[1]).reshape(rows, block, half)
    else:
        for out, parity in zip(outs, sorted(sums)):
            out[...] = sums[parity].reshape(rows, block, half)


def inverse_chunks(info, parts, tables, chunks, sums, last):
    rows, width = parts[0][0].shape[0] // 2, parts[0][0].shape[2]
    half = tables[0][0][0].shape[1]
    flat = [t for chunk in tables for pair in chunk for t in pair]
    held = sorted(sums)
    fresh = sorted(set(held) | set(piece[0] for pieces in chunks for piece in pieces))
    state = pl.BlockSpec((rows, WIDE, half), lambda i: (0, i, 0))
    state_shape = jax.ShapeDtypeStruct((rows, width, half), jnp.float32)
    if last:
        out_specs = [pl.BlockSpec((rows, WIDE, 2 * half), lambda i: (0, i, 0))]
        out_shape = [jax.ShapeDtypeStruct((rows, width, 2 * half), jnp.float32)]
    else:
        out_specs, out_shape = [state] * len(fresh), [state_shape] * len(fresh)
    in_specs = [scalars()]
    for chunk in parts:
        in_specs += [pl.BlockSpec(chunk[0].shape[:2] + (WIDE,), lambda i: (0, 0, i))] * GANG
    outs = pl.pallas_call(
        functools.partial(inverse_kernel, chunks, held, last),
        grid=(width // WIDE,),
        in_specs=in_specs
        + [pl.BlockSpec(t.shape, lambda i: (0, 0)) for t in flat]
        + [state] * len(held),
        out_specs=out_specs + [scalars()],
        out_shape=out_shape + [token_shape()],
        compiler_params=pltpu.CompilerParams(vmem_limit_bytes=VMEM_LIMIT),
        cost_estimate=cost(2 + 2 * len(chunks)),
    )(info, *[part for chunk in parts for part in chunk], *flat, *[sums[p] for p in held])
    return outs[-1], outs[0] if last else dict(zip(fresh, outs))


def shards(narrow, wide, axes, pressure, relax_freq, relax_depth):
    rows, width, n_time = pressure.shape
    n_freq = n_time // 2
    per_parity = n_freq // (2 * GANG)
    half_bins = float(n_freq // 2)
    blocks = narrow * wide // GANG

    def device(block, member):
        n, w = divmod(block * GANG + member, wide)
        return w * narrow + n if axes[0] == "wide" else n * wide + w

    swaps = [
        [(device(b, m), device(b, m ^ d)) for b in range(blocks) for m in range(GANG)]
        for d in range(GANG)
    ]
    pairs = [
        [
            (device(b + side, m), device(b + 1 - side, m))
            for b in range(first, blocks - 1, 2)
            for m in range(GANG)
            for side in range(2)
        ]
        for first in (1, 0)
    ]

    place = lax.axis_index("narrow") * wide + lax.axis_index("wide")
    block = place // GANG
    info = [place % GANG, block > 0, block < blocks - 1, (block + 1) % 2]
    info = jnp.stack([jnp.asarray(value, jnp.int32) for value in info])

    def swap(parts):
        return [parts[0]] + [lax.ppermute(parts[d], axes, swaps[d]) for d in range(1, GANG)]

    chunks = [pieces_of(chunk, per_parity) for chunk in CHUNKS]
    tables = [[transform_tables(piece, per_parity, n_time) for piece in c] for c in chunks]
    forward = [[pair[0] for pair in c] for c in tables]
    inverse = [[pair[1] for pair in c] for c in tables]
    held = [None] * len(chunks)
    inputs = (pressure, relax_freq, relax_depth)
    sums, begun, finished = {}, 0, 0
    for kernel, c in [(step[0], int(step[1:])) for step in ORDER]:
        shape = (chunks[c], per_parity, half_bins)
        if kernel == "D":
            some, begun = slice(begun, c + 1), c + 1
            info, parts = forward_chunks(info, *inputs, forward[some], chunks[some], per_parity)
            held[some] = [swap(part) for part in parts]
        elif kernel == "E":
            done, *sent, info = evolve_chunk(info, held[c], *shape)
            got = [lax.ppermute(values, axes, some) for values, some in zip(sent, pairs)]
            held[c] = (done, *sent, *got)
        elif kernel == "C":
            *parts, info = correct_chunk(info, held[c], *shape)
            held[c] = swap(parts)
        else:
            some, finished, last = slice(finished, c + 1), c + 1, c + 1 == len(chunks)
            info, sums = inverse_chunks(info, held[some], inverse[some], chunks[some], sums, last)
    return sums


def solution(mesh):
    narrow, wide = mesh.shape["narrow"], mesh.shape["wide"]
    placed = (P(("narrow", "wide"), None, None), P(), P())
    return jax.shard_map(
        functools.partial(shards, narrow, wide, tuple(mesh.axis_names)),
        mesh=mesh,
        in_specs=placed,
        out_specs=P(("narrow", "wide"), None, None),
        check_vma=False,
    )
```

```python
import functools

import jax
import jax.numpy as jnp
import ml_dtypes
import numpy as np
from jax import lax
from jax.experimental import pallas as pl
from jax.experimental.pallas import tpu as pltpu
from jax.sharding import PartitionSpec as P

SUBSTEPS = 3
WAVE_BREAKING = 0.1
RATE_TOP = 0.2

GANG = 4
SERIES = 2 * SUBSTEPS
LANES = 128
WIDE = 256
VMEM_LIMIT = 20 * 1024 * 1024
CHUNKS = (((0, 0, 4),), ((0, 4, 4),), ((1, 0, 4),), ((1, 4, 4),))
MEMBER, ABOVE, BELOW, SECOND = range(4)
SCALARS = 4
ORDER = ("D1", "D3", "E0", "E1", "C0", "E2", "C1", "E3", "I0", "C2", "I1", "C3", "I2", "I3")


def pieces_of(chunk, per_parity):
    unit = per_parity // 8
    return tuple((parity, unit * first, unit * count) for parity, first, count in chunk)


def split_high_low(table):
    high = table.astype(np.float32).astype(ml_dtypes.bfloat16)
    low = (table - high.astype(np.float64)).astype(ml_dtypes.bfloat16)
    return jnp.asarray(high), jnp.asarray(low)


def transform_tables(piece, per_parity, n_time):
    parity, first, count = piece
    member = np.arange(GANG)[:, None]
    bins = 2 * (member * per_parity + first + np.arange(count)) + parity
    half = n_time // 2
    angles = ((bins[..., None] * np.arange(half)) % n_time) * (2.0 * np.pi / n_time)
    weights = np.where(bins == 0, 1.0, 2.0)[..., None] / n_time
    forward = np.stack([np.cos(angles), -np.sin(angles)], axis=1)
    inverse = np.stack([np.cos(angles) * weights, -np.sin(angles) * weights], axis=1)
    return split_high_low(forward.reshape(-1, half)), split_high_low(inverse.reshape(-1, half))


def halves(values):
    high = values.astype(jnp.bfloat16)
    return high, (values - high.astype(jnp.float32)).astype(jnp.bfloat16)


def product(left, right, dims):
    dot = functools.partial(
        lax.dot_general, dimension_numbers=(dims, ((), ())), preferred_element_type=jnp.float32
    )
    return dot(left[0], right[0]) + (dot(left[0], right[1]) + dot(left[1], right[0]))


def partner_rows(table, member, count):
    rows = [
        table[pl.ds(pl.multiple_of((member ^ d) * 2 * count, 2 * count), 2 * count)]
        for d in range(GANG)
    ]
    return jnp.concatenate(rows, axis=0)


def pass_on(info, token):
    for place in range(SCALARS):
        token[place] = info[place]


def steepened_and_folded(wave, squared, parity):
    half = wave.shape[1] // 2
    sign = -1.0 if parity else 1.0

    def fold(values, at):
        return values[:, at : at + LANES] + sign * values[:, half + at : half + at + LANES]

    lane = lax.broadcasted_iota(jnp.int32, (wave.shape[0], LANES), 1)
    pieces = [fold(squared, at) for at in range(0, half, LANES)]
    last_early = sign * squared[:, half - LANES : half]
    first_late = squared[:, half : half + LANES]
    before = [pltpu.roll(piece, 1, 1) for piece in [last_early] + pieces]
    after = [pltpu.roll(piece, LANES - 1, 1) for piece in pieces + [first_late]]
    steep = [
        fold(wave, LANES * n)
        + WAVE_BREAKING
        * 0.25
        * (
            jnp.where(lane == LANES - 1, after[n + 1], after[n])
            - jnp.where(lane == 0, before[n], before[n + 1])
        )
        for n in range(half // LANES)
    ]
    return jnp.concatenate(steep, axis=1)


def forward_kernel(chunks, per_parity, info, freq, depth, pressure, *refs):
    n_tables = 2 * sum(len(pieces) for pieces in chunks)
    tables = iter(refs[:n_tables])
    n_outs = GANG * len(chunks)
    outs = refs[n_tables : n_tables + n_outs]
    token = refs[n_tables + n_outs]
    factors = refs[n_tables + n_outs + 1 :]
    rows, block, n_time = pressure.shape
    half = n_time // 2
    member = info[MEMBER]
    pass_on(info, token)

    @pl.when(pl.program_id(0) == 0)
    def relaxation():
        for chunk, pieces in enumerate(chunks):
            share = factors[2 * chunk].shape[1]
            place = lax.broadcasted_iota(jnp.int32, (8, LANES * pl.cdiv(share, LANES)), 1)
            for d in range(GANG):
                bins = jnp.zeros(place.shape, jnp.int32)
                offset = 0
                for parity, first, count in pieces:
                    here = 2 * ((member ^ d) * per_parity + first - offset + place) + parity
                    bins = jnp.where(place >= offset, here, bins)
                    offset += count
                bins = bins.astype(jnp.float32)
                total_re = jnp.zeros(bins.shape, jnp.float32)
                total_im = jnp.zeros(bins.shape, jnp.float32)
                for process in range(2):
                    ratio = bins / freq[process]
                    scaled = depth[process] / (1.0 + ratio * ratio)
                    total_re = total_re + scaled * ratio * ratio
                    total_im = total_im + scaled * ratio
                amplitude = jnp.exp(-total_re)
                for part, values in enumerate(
                    (amplitude * jnp.cos(total_im), -amplitude * jnp.sin(total_im))
                ):
                    column = values.T[:share, :1]
                    factors[2 * chunk + part][d] = jnp.broadcast_to(column, (share, block))

    wave = pressure[...].reshape(rows * block, n_time)
    squared = wave * wave
    folded = {}
    for parity in sorted(set(piece[0] for pieces in chunks for piece in pieces)):
        folded[parity] = halves(steepened_and_folded(wave, squared, parity))
    for chunk, pieces in enumerate(chunks):
        factor_re, factor_im = factors[2 * chunk : 2 * chunk + 2]
        offset = 0
        for parity, first, count in pieces:
            table = [partner_rows(next(tables), member, count) for _ in range(2)]
            spectrum = product(table, folded[parity], ((1,), (1,)))
            spectrum = spectrum.reshape(GANG, 2, count, rows * block)
            for d in range(GANG):
                here = slice(offset, offset + count)
                fr, fi = factor_re[d, here], factor_im[d, here]
                out = outs[GANG * chunk + d]
                for row in range(rows):
                    across = slice(row * block, (row + 1) * block)
                    real, imag = spectrum[d, 0, :, across], spectrum[d, 1, :, across]
                    out[row, here] = real * fr - imag * fi
                    out[rows + row, here] = real * fi + imag * fr
            offset += count


def cost(microseconds):
    return pl.CostEstimate(
        flops=int(microseconds * 1153000),
        bytes_accessed=int(microseconds * 3690000),
        transcendentals=0,
    )


def scalars():
    return pl.BlockSpec(memory_space=pltpu.SMEM)


def token_shape():
    return jax.ShapeDtypeStruct((SCALARS,), jnp.int32)


def in_hbm(array):
    return pltpu.with_memory_space_constraint(array, pltpu.HBM)


def forward_chunks(info, pressure, relax_freq, relax_depth, tables, chunks, per_parity):
    rows, width, n_time = pressure.shape
    flat = [in_hbm(t) for chunk in tables for pair in chunk for t in pair]
    out_specs, out_shape, scratch = [], [], []
    for pieces in chunks:
        share = sum(piece[2] for piece in pieces)
        block = pl.BlockSpec((2 * rows, share, LANES), lambda i: (0, 0, i))
        out_specs += [block] * GANG
        out_shape += [jax.ShapeDtypeStruct((2 * rows, share, width), jnp.float32)] * GANG
        scratch += [pltpu.VMEM((GANG, share, LANES), jnp.float32)] * 2
    outs = pl.pallas_call(
        functools.partial(forward_kernel, chunks, per_parity),
        grid=(width // LANES,),
        in_specs=[scalars()] * 3
        + [pl.BlockSpec((rows, LANES, n_time), lambda i: (0, i, 0))]
        + [pl.BlockSpec(t.shape, lambda i: (0, 0)) for t in flat],
        out_specs=out_specs + [scalars()],
        out_shape=out_shape + [token_shape()],
        scratch_shapes=scratch,
        compiler_params=pltpu.CompilerParams(vmem_limit_bytes=VMEM_LIMIT),
        cost_estimate=cost(2 + 2 * len(chunks)),
    )(info, in_hbm(relax_freq), in_hbm(relax_depth), in_hbm(pressure), *flat)
    return outs[-1], [outs[GANG * c : GANG * c + GANG] for c in range(len(chunks))]


def tile_of(share):
    return next(height for height in (32, 16, 8) if share % height == 0)


def bin_rates(pieces, per_parity, member, half_bins, place, shape):
    start, offset = 0, 0
    for parity, first, count in pieces:
        here = 2 * (member * per_parity + first + place - offset) + parity
        start = jnp.where(place >= offset, here, start)
        offset += count
    bins = (start + 2 * lax.broadcasted_iota(jnp.int32, shape, 0)).astype(jnp.float32)
    return RATE_TOP * jnp.minimum(bins, 1.0) * jnp.minimum(1.0, half_bins / jnp.maximum(bins, 1.0))


def lateral(height, width):
    lane = lax.broadcasted_iota(jnp.int32, (height, LANES), 1)
    first_lane, last_lane = lane == 0, lane == LANES - 1

    def apply(center):
        pieces = [center[:, at : at + LANES] for at in range(0, width, LANES)]
        left = [0.0] + [pltpu.roll(piece, 1, 1) for piece in pieces]
        right = [pltpu.roll(piece, LANES - 1, 1) for piece in pieces] + [0.0]
        sides = [
            jnp.where(first_lane, left[n], left[n + 1])
            + jnp.where(last_lane, right[n + 1], right[n])
            - 4.0 * piece
            for n, piece in enumerate(pieces)
        ]
        return jnp.concatenate(sides, axis=1)

    return apply


def evolve_kernel(pieces, per_parity, half_bins, info, *refs):
    parts = refs[:GANG]
    done, early_sent, late_sent, token, real, imag = refs[GANG:]
    member, is_second = info[MEMBER], info[SECOND] != 0
    pass_on(info, token)
    units, share, width = parts[0].shape
    rows = units // 2
    count = GANG * rows
    height = tile_of(share)
    side = lateral(height, width)

    def advance(field, other, scale):
        before, center = None, other[0]
        for row in range(count):
            after = other[row + 1] if row < count - 1 else None
            laplace = side(center)
            if before is not None:
                laplace = laplace + before
            if after is not None:
                laplace = laplace + after
            field[row] = field[row] + scale * laplace
            before, center = center, after

    def keep(place, here, field):
        top, bottom = field[0], field[count - 1]
        early_sent[place, here] = jnp.where(is_second, top, bottom)
        late_sent[place, here] = jnp.where(is_second, bottom, top)

    def tile(index, carry):
        place = pl.multiple_of(height * index, height)
        here = pl.ds(place, height)
        rate = bin_rates(pieces, per_parity, member, half_bins, place, (height, width))
        for d in range(GANG):
            first = (member ^ d) * rows
            for row in range(rows):
                real[first + row] = parts[d][row, here]
                imag[first + row] = parts[d][rows + row, here]
        for step in range(SUBSTEPS):
            keep(2 * step, here, imag)
            advance(real, imag, -rate)
            keep(2 * step + 1, here, real)
            advance(imag, real, rate)
        for row in range(count):
            done[row, here] = real[row]
            done[count + row, here] = imag[row]
        return carry

    lax.fori_loop(0, share // height, tile, 0)


def in_vmem(count):
    return [pl.BlockSpec(memory_space=pltpu.VMEM)] * count


def evolve_chunk(info, parts, pieces, per_parity, half_bins):
    units, share, width = parts[0].shape
    count = GANG * units // 2
    scratch = pltpu.VMEM((count, tile_of(share), width), jnp.float32)
    sizes = (2 * count, SERIES, SERIES)
    return pl.pallas_call(
        functools.partial(evolve_kernel, pieces, per_parity, half_bins),
        in_specs=[scalars()] + in_vmem(GANG),
        out_specs=in_vmem(3) + [scalars()],
        out_shape=[jax.ShapeDtypeStruct((n, share, width), jnp.float32) for n in sizes]
        + [token_shape()],
        scratch_shapes=[scratch, scratch],
        compiler_params=pltpu.CompilerParams(vmem_limit_bytes=VMEM_LIMIT),
        cost_estimate=cost(3.0),
    )(info, *parts)


def correct_kernel(
    pieces, per_parity, half_bins, info, done, early_sent, late_sent, early_got, late_got, *refs
):
    outs = refs[:GANG]
    token, total, *strips = refs[GANG:]
    member, is_second = info[MEMBER], info[SECOND] != 0
    pass_on(info, token)
    units, share, width = done.shape
    count = units // 2
    rows = count // GANG
    height = tile_of(share)
    side = lateral(height, width)

    def advance(field, source, edge, scale, half_step, deep):
        before, center = edge, source[0] if half_step > 0 else None
        for row in range(deep):
            after = source[row + 1] if row + 1 < half_step else None
            around = before
            if center is not None:
                around = around + side(center)
            if after is not None:
                around = around + after
            change = scale * around
            field[row] = field[row] + change if row < half_step - 1 else change
            before, center = center, after

    def tile(index, carry):
        place = pl.multiple_of(height * index, height)
        here = pl.ds(place, height)
        rate = bin_rates(pieces, per_parity, member, half_bins, place, (height, width))
        for unit in range(units):
            total[unit] = done[unit, here]
        early, late = (early_sent, early_got), (late_sent, late_got)
        edges = (
            (early, late, info[ABOVE], strips[:4], range(count)),
            (late, early, info[BELOW], strips[4:], range(count - 1, -1, -1)),
        )
        for half_step in range(SERIES):
            for if_second, if_first, flag, (near_re, near_im, far_re, far_im), _ in edges:
                own_edge, far_edge = (
                    jnp.where(is_second, one[half_step, here], two[half_step, here])
                    for one, two in zip(if_second, if_first)
                )
                of_imag = half_step % 2
                near, near_from = (near_im, near_re) if of_imag else (near_re, near_im)
                far, far_from = (far_im, far_re) if of_imag else (far_re, far_im)
                scale = rate if of_imag else -rate
                if half_step > 0:
                    own_edge = own_edge + near_from[0]
                    far_edge = far_edge + far_from[0]
                back = min(half_step + 1, SERIES - 1 - half_step)
                advance(near, near_from, far_edge, scale, half_step, half_step + 1)
                scale = scale * flag.astype(jnp.float32)
                advance(far, far_from, own_edge, scale, half_step, back)
        for _, _, _, (near_re, near_im, _, _), order in edges:
            for row in range(SERIES - 1):
                total[order[row]] = total[order[row]] + near_re[row]
            for row in range(SERIES):
                total[count + order[row]] = total[count + order[row]] + near_im[row]
        for d in range(GANG):
            first = (member ^ d) * rows
            for row in range(rows):
                outs[d][row, here] = total[first + row]
                outs[d][rows + row, here] = total[count + first + row]
        return carry

    lax.fori_loop(0, share // height, tile, 0)


def correct_chunk(info, state, pieces, per_parity, half_bins):
    units, share, width = state[0].shape
    shape = jax.ShapeDtypeStruct((units // GANG, share, width), jnp.float32)
    strip = pltpu.VMEM((SERIES, tile_of(share), width), jnp.float32)
    return pl.pallas_call(
        functools.partial(correct_kernel, pieces, per_parity, half_bins),
        in_specs=[scalars()] + in_vmem(5),
        out_specs=in_vmem(GANG) + [scalars()],
        out_shape=[shape] * GANG + [token_shape()],
        scratch_shapes=[pltpu.VMEM((units, tile_of(share), width), jnp.float32)] + [strip] * 8,
        compiler_params=pltpu.CompilerParams(vmem_limit_bytes=VMEM_LIMIT),
        cost_estimate=cost(3.5),
    )(info, *state)


def inverse_kernel(chunks, held, last, info, *refs):
    n_parts = GANG * len(chunks)
    n_tables = 2 * sum(len(pieces) for pieces in chunks)
    parts, tables = refs[:n_parts], iter(refs[n_parts : n_parts + n_tables])
    refs = refs[n_parts + n_tables :]
    prior, outs, token = dict(zip(held, refs)), refs[len(held) : -1], refs[-1]
    member = info[MEMBER]
    rows, block = parts[0].shape[0] // 2, parts[0].shape[2]
    half = outs[0].shape[2] // 2 if last else outs[0].shape[2]
    pass_on(info, token)
    sums = {parity: prior[parity][...].reshape(rows * block, half) for parity in held}
    for chunk, pieces in enumerate(chunks):
        offset = 0
        for parity, first, count in pieces:
            pair = [partner_rows(next(tables), member, count) for _ in range(2)]
            here = slice(offset, offset + count)
            packed = [
                jnp.concatenate([part[n * rows + row, here] for row in range(rows)], axis=1)
                for part in parts[GANG * chunk : GANG * chunk + GANG]
                for n in range(2)
            ]
            packed = jnp.concatenate(packed, axis=0).T
            term = product(halves(packed), pair, ((1,), (0,)))
            sums[parity] = sums[parity] + term if parity in sums else term
            offset += count
    if last:
        outs[0][:, :, :half] = (sums[0] + sums[1]).reshape(rows, block, half)
        outs[0][:, :, half:] = (sums[0] - sums[1]).reshape(rows, block, half)
    else:
        for out, parity in zip(outs, sorted(sums)):
            out[...] = sums[parity].reshape(rows, block, half)


def inverse_chunks(info, parts, tables, chunks, sums, last):
    rows, width = parts[0][0].shape[0] // 2, parts[0][0].shape[2]
    half = tables[0][0][0].shape[1]
    flat = [t for chunk in tables for pair in chunk for t in pair]
    held = sorted(sums)
    fresh = sorted(set(held) | set(piece[0] for pieces in chunks for piece in pieces))
    state = pl.BlockSpec((rows, WIDE, half), lambda i: (0, i, 0))
    state_shape = jax.ShapeDtypeStruct((rows, width, half), jnp.float32)
    if last:
        out_specs = [pl.BlockSpec((rows, WIDE, 2 * half), lambda i: (0, i, 0))]
        out_shape = [jax.ShapeDtypeStruct((rows, width, 2 * half), jnp.float32)]
    else:
        out_specs, out_shape = [state] * len(fresh), [state_shape] * len(fresh)
    in_specs = [scalars()]
    for chunk in parts:
        in_specs += [pl.BlockSpec(chunk[0].shape[:2] + (WIDE,), lambda i: (0, 0, i))] * GANG
    outs = pl.pallas_call(
        functools.partial(inverse_kernel, chunks, held, last),
        grid=(width // WIDE,),
        in_specs=in_specs
        + [pl.BlockSpec(t.shape, lambda i: (0, 0)) for t in flat]
        + [state] * len(held),
        out_specs=out_specs + [scalars()],
        out_shape=out_shape + [token_shape()],
        compiler_params=pltpu.CompilerParams(vmem_limit_bytes=VMEM_LIMIT),
        cost_estimate=cost(2 + 2 * len(chunks)),
    )(info, *[part for chunk in parts for part in chunk], *flat, *[sums[p] for p in held])
    return outs[-1], outs[0] if last else dict(zip(fresh, outs))


def shards(narrow, wide, axes, pressure, relax_freq, relax_depth):
    rows, width, n_time = pressure.shape
    n_freq = n_time // 2
    per_parity = n_freq // (2 * GANG)
    half_bins = float(n_freq // 2)
    blocks = narrow * wide // GANG

    def device(block, member):
        n, w = divmod(block * GANG + member, wide)
        return w * narrow + n if axes[0] == "wide" else n * wide + w

    swaps = [
        [(device(b, m), device(b, m ^ d)) for b in range(blocks) for m in range(GANG)]
        for d in range(GANG)
    ]
    pairs = [
        [
            (device(b + side, m), device(b + 1 - side, m))
            for b in range(first, blocks - 1, 2)
            for m in range(GANG)
            for side in range(2)
        ]
        for first in (1, 0)
    ]

    place = lax.axis_index("narrow") * wide + lax.axis_index("wide")
    block = place // GANG
    info = [place % GANG, block > 0, block < blocks - 1, (block + 1) % 2]
    info = jnp.stack([jnp.asarray(value, jnp.int32) for value in info])

    def swap(parts):
        return [parts[0]] + [lax.ppermute(parts[d], axes, swaps[d]) for d in range(1, GANG)]

    chunks = [pieces_of(chunk, per_parity) for chunk in CHUNKS]
    tables = [[transform_tables(piece, per_parity, n_time) for piece in c] for c in chunks]
    forward = [[pair[0] for pair in c] for c in tables]
    inverse = [[pair[1] for pair in c] for c in tables]
    held = [None] * len(chunks)
    inputs = (pressure, relax_freq, relax_depth)
    sums, begun, finished = {}, 0, 0
    for kernel, c in [(step[0], int(step[1:])) for step in ORDER]:
        shape = (chunks[c], per_parity, half_bins)
        if kernel == "D":
            some, begun = slice(begun, c + 1), c + 1
            info, parts = forward_chunks(info, *inputs, forward[some], chunks[some], per_parity)
            held[some] = [swap(part) for part in parts]
        elif kernel == "E":
            done, *sent, info = evolve_chunk(info, held[c], *shape)
            got = [lax.ppermute(values, axes, some) for values, some in zip(sent, pairs)]
            held[c] = (done, *sent, *got)
        elif kernel == "C":
            *parts, info = correct_chunk(info, held[c], *shape)
            held[c] = swap(parts)
        else:
            some, finished, last = slice(finished, c + 1), c + 1, c + 1 == len(chunks)
            info, sums = inverse_chunks(info, held[some], inverse[some], chunks[some], sums, last)
    return sums


def solution(mesh):
    narrow, wide = mesh.shape["narrow"], mesh.shape["wide"]
    placed = (P(("narrow", "wide"), None, None), P(), P())
    return jax.shard_map(
        functools.partial(shards, narrow, wide, tuple(mesh.axis_names)),
        mesh=mesh,
        in_specs=placed,
        out_specs=P(("narrow", "wide"), None, None),
        check_vma=False,
    )
```

```python
import functools

import jax
import jax.numpy as jnp
import ml_dtypes
import numpy as np
from jax import lax
from jax.experimental import pallas as pl
from jax.experimental.pallas import tpu as pltpu
from jax.sharding import PartitionSpec as P

SUBSTEPS = 3
WAVE_BREAKING = 0.1
RATE_TOP = 0.2

GANG = 4
SERIES = 2 * SUBSTEPS
LANES = 128
WIDE = 256
VMEM_LIMIT = 20 * 1024 * 1024
CHUNKS = (((0, 0, 4),), ((0, 4, 4),), ((1, 0, 4),), ((1, 4, 4),))
MEMBER, ABOVE, BELOW, SECOND = range(4)
SCALARS = 4
ORDER = ("D1", "D3", "E0", "E1", "C0", "E2", "C1", "E3", "I0", "C2", "I1", "C3", "I2", "I3")


def pieces_of(chunk, per_parity):
    unit = per_parity // 8
    return tuple((parity, unit * first, unit * count) for parity, first, count in chunk)


def split_high_low(table):
    high = table.astype(np.float32).astype(ml_dtypes.bfloat16)
    low = (table - high.astype(np.float64)).astype(ml_dtypes.bfloat16)
    return jnp.asarray(high), jnp.asarray(low)


def transform_tables(piece, per_parity, n_time):
    parity, first, count = piece
    member = np.arange(GANG)[:, None]
    bins = 2 * (member * per_parity + first + np.arange(count)) + parity
    half = n_time // 2
    angles = ((bins[..., None] * np.arange(half)) % n_time) * (2.0 * np.pi / n_time)
    weights = np.where(bins == 0, 1.0, 2.0)[..., None] / n_time
    forward = np.stack([np.cos(angles), -np.sin(angles)], axis=1)
    inverse = np.stack([np.cos(angles) * weights, -np.sin(angles) * weights], axis=1)
    return split_high_low(forward.reshape(-1, half)), split_high_low(inverse.reshape(-1, half))


def halves(values):
    high = values.astype(jnp.bfloat16)
    return high, (values - high.astype(jnp.float32)).astype(jnp.bfloat16)


def product(left, right, dims):
    dot = functools.partial(
        lax.dot_general, dimension_numbers=(dims, ((), ())), preferred_element_type=jnp.float32
    )
    return dot(left[0], right[0]) + (dot(left[0], right[1]) + dot(left[1], right[0]))


def partner_rows(table, member, count):
    rows = [
        table[pl.ds(pl.multiple_of((member ^ d) * 2 * count, 2 * count), 2 * count)]
        for d in range(GANG)
    ]
    return jnp.concatenate(rows, axis=0)


def pass_on(info, token):
    for place in range(SCALARS):
        token[place] = info[place]


def steepened_and_folded(wave, squared, parity):
    half = wave.shape[1] // 2
    sign = -1.0 if parity else 1.0

    def fold(values, at):
        return values[:, at : at + LANES] + sign * values[:, half + at : half + at + LANES]

    lane = lax.broadcasted_iota(jnp.int32, (wave.shape[0], LANES), 1)
    pieces = [fold(squared, at) for at in range(0, half, LANES)]
    last_early = sign * squared[:, half - LANES : half]
    first_late = squared[:, half : half + LANES]
    before = [pltpu.roll(piece, 1, 1) for piece in [last_early] + pieces]
    after = [pltpu.roll(piece, LANES - 1, 1) for piece in pieces + [first_late]]
    steep = [
        fold(wave, LANES * n)
        + WAVE_BREAKING
        * 0.25
        * (
            jnp.where(lane == LANES - 1, after[n + 1], after[n])
            - jnp.where(lane == 0, before[n], before[n + 1])
        )
        for n in range(half // LANES)
    ]
    return jnp.concatenate(steep, axis=1)


def forward_kernel(chunks, per_parity, info, freq, depth, pressure, *refs):
    n_tables = 2 * sum(len(pieces) for pieces in chunks)
    tables = iter(refs[:n_tables])
    n_outs = GANG * len(chunks)
    outs = refs[n_tables : n_tables + n_outs]
    token = refs[n_tables + n_outs]
    factors = refs[n_tables + n_outs + 1 :]
    rows, block, n_time = pressure.shape
    half = n_time // 2
    member = info[MEMBER]
    pass_on(info, token)

    @pl.when(pl.program_id(0) == 0)
    def relaxation():
        for chunk, pieces in enumerate(chunks):
            share = factors[2 * chunk].shape[1]
            place = lax.broadcasted_iota(jnp.int32, (8, LANES * pl.cdiv(share, LANES)), 1)
            for d in range(GANG):
                bins = jnp.zeros(place.shape, jnp.int32)
                offset = 0
                for parity, first, count in pieces:
                    here = 2 * ((member ^ d) * per_parity + first - offset + place) + parity
                    bins = jnp.where(place >= offset, here, bins)
                    offset += count
                bins = bins.astype(jnp.float32)
                total_re = jnp.zeros(bins.shape, jnp.float32)
                total_im = jnp.zeros(bins.shape, jnp.float32)
                for process in range(2):
                    ratio = bins / freq[process]
                    scaled = depth[process] / (1.0 + ratio * ratio)
                    total_re = total_re + scaled * ratio * ratio
                    total_im = total_im + scaled * ratio
                amplitude = jnp.exp(-total_re)
                for part, values in enumerate(
                    (amplitude * jnp.cos(total_im), -amplitude * jnp.sin(total_im))
                ):
                    column = values.T[:share, :1]
                    factors[2 * chunk + part][d] = jnp.broadcast_to(column, (share, block))

    wave = pressure[...].reshape(rows * block, n_time)
    squared = wave * wave
    folded = {}
    for parity in sorted(set(piece[0] for pieces in chunks for piece in pieces)):
        folded[parity] = halves(steepened_and_folded(wave, squared, parity))
    for chunk, pieces in enumerate(chunks):
        factor_re, factor_im = factors[2 * chunk : 2 * chunk + 2]
        offset = 0
        for parity, first, count in pieces:
            table = [partner_rows(next(tables), member, count) for _ in range(2)]
            spectrum = product(table, folded[parity], ((1,), (1,)))
            spectrum = spectrum.reshape(GANG, 2, count, rows * block)
            for d in range(GANG):
                here = slice(offset, offset + count)
                fr, fi = factor_re[d, here], factor_im[d, here]
                out = outs[GANG * chunk + d]
                for row in range(rows):
                    across = slice(row * block, (row + 1) * block)
                    real, imag = spectrum[d, 0, :, across], spectrum[d, 1, :, across]
                    out[row, here] = real * fr - imag * fi
                    out[rows + row, here] = real * fi + imag * fr
            offset += count


def cost(microseconds):
    return pl.CostEstimate(
        flops=int(microseconds * 1153000),
        bytes_accessed=int(microseconds * 3690000),
        transcendentals=0,
    )


def scalars():
    return pl.BlockSpec(memory_space=pltpu.SMEM)


def token_shape():
    return jax.ShapeDtypeStruct((SCALARS,), jnp.int32)


def in_hbm(array):
    return pltpu.with_memory_space_constraint(array, pltpu.HBM)


def forward_chunks(info, pressure, relax_freq, relax_depth, tables, chunks, per_parity):
    rows, width, n_time = pressure.shape
    flat = [in_hbm(t) for chunk in tables for pair in chunk for t in pair]
    out_specs, out_shape, scratch = [], [], []
    for pieces in chunks:
        share = sum(piece[2] for piece in pieces)
        block = pl.BlockSpec((2 * rows, share, WIDE), lambda i: (0, 0, i))
        out_specs += [block] * GANG
        out_shape += [jax.ShapeDtypeStruct((2 * rows, share, width), jnp.float32)] * GANG
        scratch += [pltpu.VMEM((GANG, share, WIDE), jnp.float32)] * 2
    outs = pl.pallas_call(
        functools.partial(forward_kernel, chunks, per_parity),
        grid=(width // WIDE,),
        in_specs=[scalars()] * 3
        + [pl.BlockSpec((rows, WIDE, n_time), lambda i: (0, i, 0))]
        + [pl.BlockSpec(t.shape, lambda i: (0, 0)) for t in flat],
        out_specs=out_specs + [scalars()],
        out_shape=out_shape + [token_shape()],
        scratch_shapes=scratch,
        compiler_params=pltpu.CompilerParams(vmem_limit_bytes=VMEM_LIMIT),
        cost_estimate=cost(2 + 2 * len(chunks)),
    )(info, in_hbm(relax_freq), in_hbm(relax_depth), in_hbm(pressure), *flat)
    return outs[-1], [outs[GANG * c : GANG * c + GANG] for c in range(len(chunks))]


def tile_of(share):
    return next(height for height in (32, 16, 8) if share % height == 0)


def bin_rates(pieces, per_parity, member, half_bins, place, shape):
    start, offset = 0, 0
    for parity, first, count in pieces:
        here = 2 * (member * per_parity + first + place - offset) + parity
        start = jnp.where(place >= offset, here, start)
        offset += count
    bins = (start + 2 * lax.broadcasted_iota(jnp.int32, shape, 0)).astype(jnp.float32)
    return RATE_TOP * jnp.minimum(bins, 1.0) * jnp.minimum(1.0, half_bins / jnp.maximum(bins, 1.0))


def lateral(height, width):
    lane = lax.broadcasted_iota(jnp.int32, (height, LANES), 1)
    first_lane, last_lane = lane == 0, lane == LANES - 1

    def apply(center):
        pieces = [center[:, at : at + LANES] for at in range(0, width, LANES)]
        left = [0.0] + [pltpu.roll(piece, 1, 1) for piece in pieces]
        right = [pltpu.roll(piece, LANES - 1, 1) for piece in pieces] + [0.0]
        sides = [
            jnp.where(first_lane, left[n], left[n + 1])
            + jnp.where(last_lane, right[n + 1], right[n])
            - 4.0 * piece
            for n, piece in enumerate(pieces)
        ]
        return jnp.concatenate(sides, axis=1)

    return apply


def evolve_kernel(pieces, per_parity, half_bins, info, *refs):
    parts = refs[:GANG]
    done, early_sent, late_sent, token, real, imag = refs[GANG:]
    member, is_second = info[MEMBER], info[SECOND] != 0
    pass_on(info, token)
    units, share, width = parts[0].shape
    rows = units // 2
    count = GANG * rows
    height = tile_of(share)
    side = lateral(height, width)

    def advance(field, other, scale):
        before, center = None, other[0]
        for row in range(count):
            after = other[row + 1] if row < count - 1 else None
            laplace = side(center)
            if before is not None:
                laplace = laplace + before
            if after is not None:
                laplace = laplace + after
            field[row] = field[row] + scale * laplace
            before, center = center, after

    def keep(place, here, field):
        top, bottom = field[0], field[count - 1]
        early_sent[place, here] = jnp.where(is_second, top, bottom)
        late_sent[place, here] = jnp.where(is_second, bottom, top)

    def tile(index, carry):
        place = pl.multiple_of(height * index, height)
        here = pl.ds(place, height)
        rate = bin_rates(pieces, per_parity, member, half_bins, place, (height, width))
        for d in range(GANG):
            first = (member ^ d) * rows
            for row in range(rows):
                real[first + row] = parts[d][row, here]
                imag[first + row] = parts[d][rows + row, here]
        for step in range(SUBSTEPS):
            keep(2 * step, here, imag)
            advance(real, imag, -rate)
            keep(2 * step + 1, here, real)
            advance(imag, real, rate)
        for row in range(count):
            done[row, here] = real[row]
            done[count + row, here] = imag[row]
        return carry

    lax.fori_loop(0, share // height, tile, 0)


def in_vmem(count):
    return [pl.BlockSpec(memory_space=pltpu.VMEM)] * count


def evolve_chunk(info, parts, pieces, per_parity, half_bins):
    units, share, width = parts[0].shape
    count = GANG * units // 2
    scratch = pltpu.VMEM((count, tile_of(share), width), jnp.float32)
    sizes = (2 * count, SERIES, SERIES)
    return pl.pallas_call(
        functools.partial(evolve_kernel, pieces, per_parity, half_bins),
        in_specs=[scalars()] + in_vmem(GANG),
        out_specs=in_vmem(3) + [scalars()],
        out_shape=[jax.ShapeDtypeStruct((n, share, width), jnp.float32) for n in sizes]
        + [token_shape()],
        scratch_shapes=[scratch, scratch],
        compiler_params=pltpu.CompilerParams(vmem_limit_bytes=VMEM_LIMIT),
        cost_estimate=cost(3.0),
    )(info, *parts)


def correct_kernel(
    pieces, per_parity, half_bins, info, done, early_sent, late_sent, early_got, late_got, *refs
):
    outs = refs[:GANG]
    token, total, *strips = refs[GANG:]
    member, is_second = info[MEMBER], info[SECOND] != 0
    pass_on(info, token)
    units, share, width = done.shape
    count = units // 2
    rows = count // GANG
    height = tile_of(share)
    side = lateral(height, width)

    def advance(field, source, edge, scale, half_step, deep):
        before, center = edge, source[0] if half_step > 0 else None
        for row in range(deep):
            after = source[row + 1] if row + 1 < half_step else None
            around = before
            if center is not None:
                around = around + side(center)
            if after is not None:
                around = around + after
            change = scale * around
            field[row] = field[row] + change if row < half_step - 1 else change
            before, center = center, after

    def tile(index, carry):
        place = pl.multiple_of(height * index, height)
        here = pl.ds(place, height)
        rate = bin_rates(pieces, per_parity, member, half_bins, place, (height, width))
        for unit in range(units):
            total[unit] = done[unit, here]
        early, late = (early_sent, early_got), (late_sent, late_got)
        edges = (
            (early, late, info[ABOVE], strips[:4], range(count)),
            (late, early, info[BELOW], strips[4:], range(count - 1, -1, -1)),
        )
        for half_step in range(SERIES):
            for if_second, if_first, flag, (near_re, near_im, far_re, far_im), _ in edges:
                own_edge, far_edge = (
                    jnp.where(is_second, one[half_step, here], two[half_step, here])
                    for one, two in zip(if_second, if_first)
                )
                of_imag = half_step % 2
                near, near_from = (near_im, near_re) if of_imag else (near_re, near_im)
                far, far_from = (far_im, far_re) if of_imag else (far_re, far_im)
                scale = rate if of_imag else -rate
                if half_step > 0:
                    own_edge = own_edge + near_from[0]
                    far_edge = far_edge + far_from[0]
                back = min(half_step + 1, SERIES - 1 - half_step)
                advance(near, near_from, far_edge, scale, half_step, half_step + 1)
                scale = scale * flag.astype(jnp.float32)
                advance(far, far_from, own_edge, scale, half_step, back)
        for _, _, _, (near_re, near_im, _, _), order in edges:
            for row in range(SERIES - 1):
                total[order[row]] = total[order[row]] + near_re[row]
            for row in range(SERIES):
                total[count + order[row]] = total[count + order[row]] + near_im[row]
        for d in range(GANG):
            first = (member ^ d) * rows
            for row in range(rows):
                outs[d][row, here] = total[first + row]
                outs[d][rows + row, here] = total[count + first + row]
        return carry

    lax.fori_loop(0, share // height, tile, 0)


def correct_chunk(info, state, pieces, per_parity, half_bins):
    units, share, width = state[0].shape
    shape = jax.ShapeDtypeStruct((units // GANG, share, width), jnp.float32)
    strip = pltpu.VMEM((SERIES, tile_of(share), width), jnp.float32)
    return pl.pallas_call(
        functools.partial(correct_kernel, pieces, per_parity, half_bins),
        in_specs=[scalars()] + in_vmem(5),
        out_specs=in_vmem(GANG) + [scalars()],
        out_shape=[shape] * GANG + [token_shape()],
        scratch_shapes=[pltpu.VMEM((units, tile_of(share), width), jnp.float32)] + [strip] * 8,
        compiler_params=pltpu.CompilerParams(vmem_limit_bytes=VMEM_LIMIT),
        cost_estimate=cost(3.5),
    )(info, *state)


def inverse_kernel(chunks, held, last, info, *refs):
    n_parts = GANG * len(chunks)
    n_tables = 2 * sum(len(pieces) for pieces in chunks)
    parts, tables = refs[:n_parts], iter(refs[n_parts : n_parts + n_tables])
    refs = refs[n_parts + n_tables :]
    prior, outs, token = dict(zip(held, refs)), refs[len(held) : -1], refs[-1]
    member = info[MEMBER]
    rows, block = parts[0].shape[0] // 2, parts[0].shape[2]
    half = outs[0].shape[2] // 2 if last else outs[0].shape[2]
    pass_on(info, token)
    sums = {parity: prior[parity][...].reshape(rows * block, half) for parity in held}
    for chunk, pieces in enumerate(chunks):
        offset = 0
        for parity, first, count in pieces:
            pair = [partner_rows(next(tables), member, count) for _ in range(2)]
            here = slice(offset, offset + count)
            packed = [
                jnp.concatenate([part[n * rows + row, here] for row in range(rows)], axis=1)
                for part in parts[GANG * chunk : GANG * chunk + GANG]
                for n in range(2)
            ]
            packed = jnp.concatenate(packed, axis=0).T
            term = product(halves(packed), pair, ((1,), (0,)))
            sums[parity] = sums[parity] + term if parity in sums else term
            offset += count
    if last:
        outs[0][:, :, :half] = (sums[0] + sums[1]).reshape(rows, block, half)
        outs[0][:, :, half:] = (sums[0] - sums[1]).reshape(rows, block, half)
    else:
        for out, parity in zip(outs, sorted(sums)):
            out[...] = sums[parity].reshape(rows, block, half)


def inverse_chunks(info, parts, tables, chunks, sums, last):
    rows, width = parts[0][0].shape[0] // 2, parts[0][0].shape[2]
    half = tables[0][0][0].shape[1]
    flat = [t for chunk in tables for pair in chunk for t in pair]
    held = sorted(sums)
    fresh = sorted(set(held) | set(piece[0] for pieces in chunks for piece in pieces))
    state = pl.BlockSpec((rows, WIDE, half), lambda i: (0, i, 0))
    state_shape = jax.ShapeDtypeStruct((rows, width, half), jnp.float32)
    if last:
        out_specs = [pl.BlockSpec((rows, WIDE, 2 * half), lambda i: (0, i, 0))]
        out_shape = [jax.ShapeDtypeStruct((rows, width, 2 * half), jnp.float32)]
    else:
        out_specs, out_shape = [state] * len(fresh), [state_shape] * len(fresh)
    in_specs = [scalars()]
    for chunk in parts:
        in_specs += [pl.BlockSpec(chunk[0].shape[:2] + (WIDE,), lambda i: (0, 0, i))] * GANG
    outs = pl.pallas_call(
        functools.partial(inverse_kernel, chunks, held, last),
        grid=(width // WIDE,),
        in_specs=in_specs
        + [pl.BlockSpec(t.shape, lambda i: (0, 0)) for t in flat]
        + [state] * len(held),
        out_specs=out_specs + [scalars()],
        out_shape=out_shape + [token_shape()],
        compiler_params=pltpu.CompilerParams(vmem_limit_bytes=VMEM_LIMIT),
        cost_estimate=cost(2 + 2 * len(chunks)),
    )(info, *[part for chunk in parts for part in chunk], *flat, *[sums[p] for p in held])
    return outs[-1], outs[0] if last else dict(zip(fresh, outs))


def shards(narrow, wide, axes, pressure, relax_freq, relax_depth):
    rows, width, n_time = pressure.shape
    n_freq = n_time // 2
    per_parity = n_freq // (2 * GANG)
    half_bins = float(n_freq // 2)
    blocks = narrow * wide // GANG

    def device(block, member):
        n, w = divmod(block * GANG + member, wide)
        return w * narrow + n if axes[0] == "wide" else n * wide + w

    swaps = [
        [(device(b, m), device(b, m ^ d)) for b in range(blocks) for m in range(GANG)]
        for d in range(GANG)
    ]
    pairs = [
        [
            (device(b + side, m), device(b + 1 - side, m))
            for b in range(first, blocks - 1, 2)
            for m in range(GANG)
            for side in range(2)
        ]
        for first in (1, 0)
    ]

    place = lax.axis_index("narrow") * wide + lax.axis_index("wide")
    block = place // GANG
    info = [place % GANG, block > 0, block < blocks - 1, (block + 1) % 2]
    info = jnp.stack([jnp.asarray(value, jnp.int32) for value in info])

    def swap(parts):
        return [parts[0]] + [lax.ppermute(parts[d], axes, swaps[d]) for d in range(1, GANG)]

    chunks = [pieces_of(chunk, per_parity) for chunk in CHUNKS]
    tables = [[transform_tables(piece, per_parity, n_time) for piece in c] for c in chunks]
    forward = [[pair[0] for pair in c] for c in tables]
    inverse = [[pair[1] for pair in c] for c in tables]
    held = [None] * len(chunks)
    inputs = (pressure, relax_freq, relax_depth)
    sums, begun, finished = {}, 0, 0
    for kernel, c in [(step[0], int(step[1:])) for step in ORDER]:
        shape = (chunks[c], per_parity, half_bins)
        if kernel == "D":
            some, begun = slice(begun, c + 1), c + 1
            info, parts = forward_chunks(info, *inputs, forward[some], chunks[some], per_parity)
            held[some] = [swap(part) for part in parts]
        elif kernel == "E":
            done, *sent, info = evolve_chunk(info, held[c], *shape)
            got = [lax.ppermute(values, axes, some) for values, some in zip(sent, pairs)]
            held[c] = (done, *sent, *got)
        elif kernel == "C":
            *parts, info = correct_chunk(info, held[c], *shape)
            held[c] = swap(parts)
        else:
            some, finished, last = slice(finished, c + 1), c + 1, c + 1 == len(chunks)
            info, sums = inverse_chunks(info, held[some], inverse[some], chunks[some], sums, last)
    return sums


def solution(mesh):
    narrow, wide = mesh.shape["narrow"], mesh.shape["wide"]
    placed = (P(("narrow", "wide"), None, None), P(), P())
    return jax.shard_map(
        functools.partial(shards, narrow, wide, tuple(mesh.axis_names)),
        mesh=mesh,
        in_specs=placed,
        out_specs=P(("narrow", "wide"), None, None),
        check_vma=False,
    )
```
